512 devices in a mesh: lat: 128 (over y, z, core), ch: 4 (over x).
Axes of the slice: x: 4, y: 4, z: 16, core: 2. Of those that a mesh axis runs over, the one named last changes fastest.
Arguments:
- features: bfloat16 [128, 512, 1440], P('ch', 'lat'), may hold values from -6 to 6
- projection: float32 [128, 512], replicated, may hold values from -0.25 to 0.25
- synthesis: float32 [512, 128], replicated, may hold values from -0.5 to 0.5
- mode_weights: bfloat16 [128, 2, 128, 128], P('lat'), may hold values from -0.375 to 0.375
- skip_weights: bfloat16 [128, 128], replicated, may hold values from -0.5 to 0.5
- cotangent: bfloat16 [128, 512, 1440], P('ch', 'lat'), may hold values from -6 to 6
Outputs:
- output: bfloat16 [128, 512, 1440], P('ch', 'lat')
- grad_features: bfloat16 [128, 512, 1440], P('ch', 'lat')
- grad_weights: float32 [128, 2, 128, 128], P('lat', None, None, 'ch')
- grad_skip: float32 [128, 128], P(None, 'ch')
The draws below stay inside these ranges and needn't reach their ends.
All inputs are finite; a program needn't handle non-finite values.
Results may differ from the reference program's by a relative error of at most 0.018.
Values may be sent and summed in bfloat16 or wider, within the bound.
A program may use at most 64 MiB of HBM per device.

```python
import math
import jax
import jax.numpy as jnp
from jax import lax

C = 128
NLON = 1440
M = 64
L = 128
NLAT = 512


def shard_levels(key, shape, shards, smallest, high):
    gain, own = 1.0, jax.random.fold_in(key, 6)
    for dim, parts in shards:
        draws = jnp.exp(jax.random.uniform(jax.random.fold_in(own, dim), (parts,), jnp.float32, smallest / len(shards), high / len(shards)))
        gain = gain * jnp.repeat(draws, shape[dim] // parts).reshape([-1 if axis == dim else 1 for axis in range(len(shape))])
    return gain


def gaussian(key, extent, deviation, bound, cuts=(), kind=jnp.bfloat16):
    result = deviation * jax.random.normal(key, extent, jnp.float32)
    if cuts:
        result = result * shard_levels(key, extent, cuts, -0.22, 0.18)
    return jnp.clip(result, -bound, bound).astype(kind)


def setup_inputs(seed: int = 0) -> dict:
    keys = jax.random.split(jax.random.key(seed), 7)
    return {
        "features": gaussian(keys[0], (C, NLAT, NLON), 1.0, 6.0, ((0, 4), (1, 128))),
        "projection": gaussian(keys[1], (L, NLAT), NLAT ** -0.5, 0.25, (), jnp.float32),
        "synthesis": gaussian(keys[2], (NLAT, L), L ** -0.5, 0.5, (), jnp.float32),
        "mode_weights": gaussian(keys[3], (L, 2, C, C), (2 * C) ** -0.5, 0.375, ((0, 128),)),
        "skip_weights": gaussian(keys[4], (C, C), C ** -0.5, 0.5),
        "cotangent": gaussian(keys[5], (C, NLAT, NLON), 1.0, 6.0, ((0, 4), (1, 128))),
    }


def build_tables(length, mode_count):
    column = jnp.arange(length, dtype=jnp.int32)
    mode_index = jnp.arange(mode_count, dtype=jnp.int32)
    phase_turns = column[:, None] * mode_index[None, :] % length
    phases = phase_turns.astype(jnp.float32) * (2.0 * math.pi / length)
    factor = 1.0 / math.sqrt(length)
    doubling = jnp.where(mode_index == 0, 1.0, 2.0).astype(jnp.float32)
    forward_table = (jnp.concatenate([jnp.cos(phases), -jnp.sin(phases)], 1) * factor).astype(jnp.bfloat16)
    inverse_table = (jnp.concatenate([jnp.cos(phases) * doubling, -jnp.sin(phases) * doubling], 1) * factor).T.astype(jnp.bfloat16)
    return (forward_table, inverse_table)

def widen(values):
    return values.astype(jnp.float32)

def contract(form, left, right):
    return jnp.einsum(form, widen(left), widen(right), precision=lax.Precision.HIGHEST)

def reference(features, projection, synthesis, mode_weights, skip_weights, cotangent):
    forward_table, inverse_table = build_tables(NLON, M)
    x_modes = contract('can,nj->caj', features, forward_table)
    spectral = contract('la,caj->lcj', projection, x_modes).astype(jnp.bfloat16)
    w_real = mode_weights[:, 0]
    w_imag = mode_weights[:, 1]
    s_real = spectral[:, :, :M]
    s_imag = spectral[:, :, M:]
    out_real = contract('lco,lcm->lom', w_real, s_real) - contract('lco,lcm->lom', w_imag, s_imag)
    out_imag = contract('lco,lcm->lom', w_real, s_imag) + contract('lco,lcm->lom', w_imag, s_real)
    mixed = jnp.concatenate([out_real, out_imag], 2).astype(jnp.bfloat16)
    v_modes = contract('al,loj->oaj', synthesis, mixed).astype(jnp.bfloat16)
    spectral_field = contract('oaj,jn->oan', v_modes, inverse_table)
    skip_field = contract('co,can->oan', skip_weights, features)
    activation_in = spectral_field + skip_field
    output_field, pullback = jax.vjp(jax.nn.gelu, activation_in)
    g_pre = pullback(widen(cotangent))[0].astype(jnp.bfloat16)
    g_vmodes = contract('oan,jn->oaj', g_pre, inverse_table)
    g_mixed = contract('al,oaj->loj', synthesis, g_vmodes).astype(jnp.bfloat16)
    g_real = g_mixed[:, :, :M]
    g_imag = g_mixed[:, :, M:]
    back_real = contract('lco,lom->lcm', w_real, g_real) + contract('lco,lom->lcm', w_imag, g_imag)
    back_imag = contract('lco,lom->lcm', w_real, g_imag) - contract('lco,lom->lcm', w_imag, g_real)
    g_spectral = jnp.concatenate([back_real, back_imag], 2).astype(jnp.bfloat16)
    grad_zero = contract('lcm,lom->lco', s_real, g_real) + contract('lcm,lom->lco', s_imag, g_imag)
    grad_one = contract('lcm,lom->lco', s_real, g_imag) - contract('lcm,lom->lco', s_imag, g_real)
    grad_weights = jnp.stack([grad_zero, grad_one], 1) / math.sqrt(2 * M)
    g_xmodes = contract('la,lcj->caj', projection, g_spectral).astype(jnp.bfloat16)
    g_spectral_field = contract('caj,nj->can', g_xmodes, forward_table)
    g_skip = contract('co,oan->can', skip_weights, g_pre)
    grad_features = (g_spectral_field + g_skip).astype(jnp.bfloat16)
    grad_skip = contract('can,oan->co', features, g_pre) / math.sqrt(NLAT * NLON)
    return (output_field.astype(jnp.bfloat16), grad_features, grad_weights, grad_skip)
```

```python
import math

import jax
import jax.numpy as jnp
import numpy as np
from jax import lax
from jax.experimental import pallas as pl
from jax.experimental.pallas import tpu as pltpu
from jax.sharding import PartitionSpec as P

MESH = pl.DeviceIdType.MESH
F32 = jnp.float32
BF16 = jnp.bfloat16

M = 64
NLON = 1440
C = 128
X, Y, Z, K = 4, 4, 16, 2
B = Y * K
PLANE = X * B
GROUP = C // X
ROWS = 4
CHUNK = 16


def fourier_table():
    column = np.arange(NLON)
    mode = np.arange(M)
    phase = (mode[:, None] * column[None, :] % NLON) * (2.0 * math.pi / NLON)
    table = np.concatenate([np.cos(phase), -np.sin(phase)], 0) / math.sqrt(NLON)
    return jnp.asarray(table.astype(np.float32), BF16)


def shuffle_table():
    table = np.zeros((ROWS, GROUP, ROWS, ROWS, ROWS, GROUP), np.float32)
    for jj in range(4):
        for c in range(GROUP):
            for a in range(ROWS):
                table[jj, c, a, a, jj, c] = 1
    return jnp.asarray(table.reshape(512, 512), BF16)


def row_table():
    table = np.zeros((Z, X, B, C), np.float32)
    for z in range(Z):
        for b in range(B):
            table[z, :, b, (b // K) * Z * K + z * K + b % K] = 1
    return jnp.asarray(table.reshape(512, C), BF16)


def iota(shape, dim):
    return lax.broadcasted_iota(jnp.int32, shape, dim)


def dot(left, right):
    return jnp.dot(left, right, preferred_element_type=F32)


def dot_t(left, right):
    return lax.dot_general(left, right, (((1,), (1,)), ((), ())), preferred_element_type=F32)


def onehot(mask):
    return jnp.where(mask, 1.0, 0.0).astype(BF16)


def swap_blocks(v):
    lane = iota((8, 128), 1) // 32
    parts = [v[8 * p : 8 * p + 8] for p in range(4)]
    rows = []
    for q in range(4):
        row = parts[q]
        for p in range(4):
            if p != q:
                row = jnp.where(lane == p, pltpu.roll(parts[p], ((p - q) * 32) % 128, 1), row)
        rows.append(row)
    return jnp.concatenate(rows, 0)


def kernel(
    f_ref, cot_ref, p_ref, s_ref, w_ref, skip_ref, tt_ref, shuffle_ref, pick_ref,
    out_ref, gf_ref, gw_ref, gk_ref,
    fall, gall, wall, act, pbig, sbig, pbig_t, sbig_t, kron1, kron2,
    xs, xr, ys, yr, ms, mr, vs, vr,
    bxs, bxr, bys, byr, bms, bmr, bvs, bvr,
    gws, gwr, k1s, k1r, k2s, k2r, k3r,
    send, recv, local,
):
    lat = lax.axis_index("lat")
    x = lax.axis_index("ch")
    y, z, core = lat // (Z * K), (lat // K) % Z, lat % K
    b = y * K + core
    me = x * B + b

    def plane_device(s):
        bb = s % B
        return ((bb // K) * (Z * K) + z * K + bb % K, s // B)

    def z_device(zz):
        return (y * (Z * K) + zz * K + core, x)

    def remote(src, dst, slot, device):
        return pltpu.make_async_remote_copy(
            src_ref=src, dst_ref=dst, send_sem=send.at[slot], recv_sem=recv.at[slot],
            device_id=device, device_id_type=MESH,
        )

    def to_plane(slot, src, dst):
        @pl.loop(1, PLANE)
        def _(i):
            s = lax.rem(me + i, PLANE)
            remote(src.at[s], dst.at[me], slot, plane_device(s)).start()

        dst[me] = src[me]

    def to_column(slot, src, dst, indexed):
        @pl.loop(1, Z)
        def _(i):
            zz = lax.rem(z + i, Z)
            remote(src.at[zz] if indexed else src, dst.at[z], slot, z_device(zz)).start()

        dst[z] = src[z] if indexed else src[...]

    def wait_recv(slot, dst, count):
        part = dst.at[pl.ds(0, count)]
        pltpu.make_async_copy(part, part, recv.at[slot]).wait()

    def wait_send(slot, dst, count):
        part = dst.at[pl.ds(0, count)]
        pltpu.make_async_copy(part, part, send.at[slot]).wait()

    barrier = pltpu.get_barrier_semaphore()

    @pl.loop(1, PLANE)
    def _(i):
        pl.semaphore_signal(
            barrier, inc=1, device_id=plane_device(lax.rem(me + i, PLANE)), device_id_type=MESH
        )

    @pl.loop(1, Z)
    def _(i):
        pl.semaphore_signal(
            barrier, inc=1, device_id=z_device(lax.rem(z + i, Z)), device_id_type=MESH
        )

    def spread(values, dst):
        rounded = values.astype(BF16)
        cat = jnp.concatenate([rounded[32 * jj : 32 * jj + 32] for jj in range(4)], 1)
        for a in range(ROWS):
            dst[:, a, :] = dot(cat, shuffle_ref[:, 128 * a : 128 * a + 128])

    def collect(src):
        cat = jnp.concatenate([src[:, a, :] for a in range(ROWS)], 1).astype(BF16)
        wide = dot_t(cat, shuffle_ref[...])
        tall = jnp.concatenate([wide[:, 128 * jj : 128 * jj + 128] for jj in range(4)], 0)
        return tall.T

    def partial_sums(big, src, dst):
        rows = jnp.concatenate([src[:, a, :] for a in range(ROWS)], 0).astype(BF16)
        dst[...] = dot(big[...], rows).astype(BF16).reshape(Z, 32, 128)

    def total(src):
        acc = src[0].astype(F32)
        for zz in range(1, Z):
            acc = acc + src[zz].astype(F32)
        return swap_blocks(acc)

    def expand_rows(big, src, dst):
        v = dot(big[...], src[...].reshape(512, 128))
        for a in range(ROWS):
            dst[:, a, :] = swap_blocks(v[32 * a : 32 * a + 32])

    def mode_rows(values, mode):
        return jnp.where(iota((32, 128), 0) % 8 == mode, values, 0.0).astype(BF16)

    spread(dot_t(tt_ref[...], f_ref[...]), xs)
    pl.semaphore_wait(barrier, PLANE - 1 + Z - 1)

    to_plane(0, xs, xr)

    def gather_x(slot, src, dst):
        @pl.loop(1, X)
        def _(i):
            remote(src, dst.at[x], slot, (lat, lax.rem(x + i, X))).start()

        dst[x] = src[...]

    @pl.loop(1, B)
    def _(i):
        bb = lax.rem(b + i, B)
        remote(w_ref.at[0], wall.at[b], 1, plane_device(x * B + bb)).start()

    wall[b] = w_ref[0]
    gather_x(2, f_ref, fall)

    row = iota((128, 512), 0)
    bb = row % B
    pick_a = onehot(
        iota((128, 512), 1) == (bb // K) * (Z * K * ROWS) + (z * K + bb % K) * ROWS + row // 32
    )
    p_rows = dot_t(pick_a, p_ref[...].astype(BF16)).astype(BF16)
    s_rows = dot(pick_a, s_ref[...].astype(BF16)).astype(BF16)
    same = (iota((512, 128), 0) // 8) % 4 == (iota((512, 128), 1) // 8) % 4
    same_t = (iota((128, 512), 0) // 8) % 4 == (iota((128, 512), 1) // 8) % 4
    pick = pick_ref[...]
    pbig[...] = jnp.where(same, dot_t(pick, p_rows), 0.0).astype(BF16)
    sbig[...] = jnp.where(same_t, dot_t(s_rows, pick), 0.0).astype(BF16)

    wait_recv(0, xr, PLANE - 1)
    partial_sums(pbig, xr, ys)
    to_column(3, ys, yr, True)

    sbig_t[...] = jnp.where(same, dot_t(pick, s_rows), 0.0).astype(BF16)
    pbig_t[...] = jnp.where(same_t, dot_t(p_rows, pick), 0.0).astype(BF16)
    own = onehot(iota((128, 128), 1) == x * GROUP + iota((128, 128), 0) // ROWS)
    each = onehot(iota((128, 512), 0) == iota((128, 512), 1) // ROWS)
    same_row = iota((128, 512), 0) % ROWS == iota((128, 512), 1) % ROWS
    skip = skip_ref[...]
    kron1[...] = jnp.where(same_row, dot(dot_t(own, skip).astype(BF16), each), 0.0).astype(BF16)
    kron2[...] = jnp.where(same_row, dot(dot(own, skip).astype(BF16), each), 0.0).astype(BF16)

    wait_recv(1, wall, B - 1)
    wait_recv(3, yr, Z - 1)
    spectral = total(yr).astype(BF16).astype(F32)
    w0 = wall[:, 0].reshape(B * C, C)
    w1 = wall[:, 1].reshape(B * C, C)
    wide = jnp.concatenate([mode_rows(spectral, m) for m in range(B)], 1)
    r0, r1 = dot(wide, w0), dot(wide, w1)
    mixed = jnp.concatenate([r0[:16] - r1[16:], r0[16:] + r1[:16]], 0)
    ms[...] = mixed.astype(BF16)
    to_column(4, ms, mr, False)
    for jj in range(4):
        gws[:, jj, :] = spectral[8 * jj : 8 * jj + 8]

    wait_recv(2, fall, X - 1)
    acc = dot(kron1[:, 0:128], fall[0])
    for g in range(1, X):
        acc = acc + dot(kron1[:, 128 * g : 128 * g + 128], fall[g])
    act[...] = acc

    wait_recv(4, mr, Z - 1)
    expand_rows(sbig, mr, vs)
    to_plane(5, vs, vr)

    col = iota((128, 128), 1) % M
    doubling = jnp.where(col == 0, 1.0, 2.0)
    wait_recv(5, vr, PLANE - 1)
    v_modes = (collect(vr) * doubling).astype(BF16)
    act[...] += dot(v_modes, tt_ref[...])

    scale = math.sqrt(2.0 / math.pi)

    g_ref = gall.at[x]

    @pl.loop(0, 128 // CHUNK)
    def _(i):
        rows = pl.ds(pl.multiple_of(i * CHUNK, CHUNK), CHUNK)
        u = act[rows, :]
        square = u * u
        t = jnp.tanh(scale * u * (1.0 + 0.044715 * square))
        cdf = 0.5 * (1.0 + t)
        out_ref[rows, :] = (u * cdf).astype(BF16)
        slope = cdf + 0.5 * u * (1.0 - t * t) * (scale * (1.0 + 3 * 0.044715 * square))
        g_ref[rows, :] = (cot_ref[rows, :].astype(F32) * slope).astype(BF16)

    g_pre = g_ref[...]
    row = iota((128, 128), 0) % M
    doubling_t = jnp.where(row == 0, 1.0, 2.0)
    spread(dot_t(tt_ref[...], g_pre) * doubling_t, bxs)
    to_plane(6, bxs, bxr)

    @pl.loop(1, X)
    def _(i):
        remote(g_ref, gall.at[x], 7, (lat, lax.rem(x + i, X))).start()

    wait_recv(6, bxr, PLANE - 1)
    partial_sums(sbig_t, bxr, bys)
    to_column(8, bys, byr, True)

    same_lane = iota((128, 128), 0) % ROWS == iota((128, 128), 1) % ROWS
    term = jnp.zeros((128, 128), F32)
    for g in range(X):
        full = jnp.where(same_lane, dot_t(g_pre, fall[g]), 0.0)
        lanes = jnp.where(iota((128, 128), 1) == GROUP * g + iota((128, 128), 0) // ROWS, 1.0, 0.0)
        term = term + jnp.dot(
            full, lanes, precision=lax.Precision.HIGHEST, preferred_element_type=F32
        )
    fold = jnp.where(iota((32, 128), 0) == iota((32, 128), 1) // ROWS, 1.0, 0.0)
    term = jnp.dot(fold, term, precision=lax.Precision.HIGHEST, preferred_element_type=F32)
    for i in range(ROWS):
        k1s[:, i, :] = term[8 * i : 8 * i + 8]

    @pl.loop(1, B)
    def _(i):
        bb = lax.rem(b + i, B)
        remote(k1s.at[bb], k1r.at[b], 9, plane_device(x * B + bb)).start()

    k1r[b] = k1s[b]

    wait_recv(8, byr, Z - 1)
    g_mixed = total(byr).astype(BF16).astype(F32)
    r0 = jnp.zeros((32, C), F32)
    r1 = jnp.zeros((32, C), F32)
    for m in range(B):
        masked = mode_rows(g_mixed, m)
        r0 = r0 + dot_t(masked, wall[m, 0])
        r1 = r1 + dot_t(masked, wall[m, 1])
    g_spectral = jnp.concatenate([r0[:16] + r1[16:], r0[16:] - r1[:16]], 0)
    bms[...] = g_spectral.astype(BF16)
    to_column(10, bms, bmr, False)

    for jj in range(4):
        gws[:, 4 + jj, :] = g_mixed[8 * jj : 8 * jj + 8]

    @pl.loop(1, PLANE)
    def _(i):
        s = lax.rem(me + i, PLANE)
        remote(gws.at[s % B], gwr.at[me], 11, plane_device(s)).start()

    gwr[me] = gws[b]

    wait_recv(9, k1r, B - 1)
    acc = k1r[0]
    for i in range(1, B):
        acc = acc + k1r[i]
    k2s[...] = acc

    @pl.loop(1, Z)
    def _(i):
        remote(k2s, k2r.at[z], 12, z_device(lax.rem(z + i, Z))).start()

    k2r[z] = k2s[...]

    wait_recv(10, bmr, Z - 1)
    expand_rows(pbig_t, bmr, bvs)
    to_plane(13, bvs, bvr)

    wait_recv(7, gall, X - 1)
    acc = dot(kron2[:, 0:128], gall[0])
    for g in range(1, X):
        acc = acc + dot(kron2[:, 128 * g : 128 * g + 128], gall[g])
    act[...] = acc

    wait_recv(12, k2r, Z - 1)
    acc = k2r[0]
    for i in range(1, Z):
        acc = acc + k2r[i]
    k3r[b] = acc * (1.0 / math.sqrt(Y * Z * K * ROWS * NLON))

    @pl.loop(1, B)
    def _(i):
        bb = lax.rem(b + i, B)
        remote(k3r.at[b], k3r.at[b], 14, plane_device(x * B + bb)).start()

    wait_recv(11, gwr, PLANE - 1)
    s_all = jnp.concatenate([gwr[:, jj, :] for jj in range(4)], 0).T.astype(BF16)
    g_all = jnp.concatenate([gwr[:, 4 + jj, :] for jj in range(4)], 0).astype(BF16)
    pick_o = onehot(iota((128, GROUP), 0) == x * GROUP + iota((128, GROUP), 1))
    g_own = dot(g_all, pick_o)
    g_turn = jnp.concatenate([g_own[64:], -g_own[:64]], 0)
    gw_ref[0, 0] = dot(s_all, g_own.astype(BF16)) * (1.0 / math.sqrt(2 * M))
    gw_ref[0, 1] = dot(s_all, g_turn.astype(BF16)) * (1.0 / math.sqrt(2 * M))

    wait_recv(13, bvr, PLANE - 1)
    gf_ref[...] = (act[...] + dot(collect(bvr).astype(BF16), tt_ref[...])).astype(BF16)

    wait_recv(14, k3r, B - 1)
    gk = jnp.concatenate([k3r[:, i, :] for i in range(ROWS)], 0)
    gk_ref[...] = gk.T

    wait_send(0, xs, PLANE - 1)
    wait_send(1, wall, B - 1)
    wait_send(2, fall, X - 1)
    wait_send(3, ys, Z - 1)
    wait_send(4, mr, Z - 1)
    wait_send(5, vs, PLANE - 1)
    wait_send(6, bxs, PLANE - 1)
    wait_send(7, gall, X - 1)
    wait_send(8, bys, Z - 1)
    wait_send(9, k1s, B - 1)
    wait_send(10, bmr, Z - 1)
    wait_send(11, gwr, PLANE - 1)
    wait_send(12, k2r, Z - 1)
    wait_send(13, bvs, PLANE - 1)
    wait_send(14, k3r, B - 1)


def on_device(features, projection, synthesis, mode_weights, skip_weights, cotangent):
    vmem = pl.BlockSpec(memory_space=pltpu.VMEM)
    plane = pltpu.VMEM((PLANE, ROWS, 128), F32)
    column = pltpu.VMEM((Z, 32, 128), BF16)
    one = pltpu.VMEM((32, 128), BF16)
    tall = pltpu.VMEM((512, 128), BF16)
    flat = pltpu.VMEM((128, 512), BF16)
    field = pltpu.VMEM((X, GROUP * ROWS, NLON), BF16)
    phases = [plane, plane, column, column, one, column, plane, plane]
    out, grad_features, grad_weights, grad_skip = pl.pallas_call(
        kernel,
        out_shape=(
            jax.ShapeDtypeStruct((GROUP * ROWS, NLON), BF16),
            jax.ShapeDtypeStruct((GROUP * ROWS, NLON), BF16),
            jax.ShapeDtypeStruct((1, 2, C, GROUP), F32),
            jax.ShapeDtypeStruct((C, GROUP), F32),
        ),
        in_specs=[vmem] * 9,
        out_specs=[vmem] * 4,
        scratch_shapes=[
            field,
            field,
            pltpu.VMEM((B, 2, C, C), BF16),
            pltpu.VMEM((GROUP * ROWS, NLON), F32),
            tall, flat, flat, tall, flat, flat,
            *phases,
            *phases,
            pltpu.VMEM((B, 8, 128), F32),
            pltpu.VMEM((PLANE, 8, 128), F32),
            pltpu.VMEM((B, ROWS, 128), F32),
            pltpu.VMEM((B, ROWS, 128), F32),
            pltpu.VMEM((ROWS, 128), F32),
            pltpu.VMEM((Z, ROWS, 128), F32),
            pltpu.VMEM((B, ROWS, 128), F32),
            pltpu.SemaphoreType.DMA((15,)),
            pltpu.SemaphoreType.DMA((15,)),
            pltpu.SemaphoreType.DMA,
        ],
        compiler_params=pltpu.CompilerParams(
            collective_id=0, has_side_effects=True, vmem_limit_bytes=40 * 1024 * 1024
        ),
    )(
        features.reshape(GROUP * ROWS, NLON),
        cotangent.reshape(GROUP * ROWS, NLON),
        projection,
        synthesis,
        mode_weights,
        skip_weights,
        fourier_table(),
        shuffle_table(),
        row_table(),
    )
    shape = features.shape
    return (out.reshape(shape), grad_features.reshape(shape), grad_weights, grad_skip)


def solution(mesh):
    placed = (P("ch", "lat", None), P(), P(), P("lat", None, None, None), P(), P("ch", "lat", None))
    return jax.shard_map(
        on_device,
        mesh=mesh,
        in_specs=placed,
        out_specs=(
            P("ch", "lat", None),
            P("ch", "lat", None),
            P("lat", None, None, "ch"),
            P(None, "ch"),
        ),
        check_vma=False,
    )
```

```python
import math

import jax
import jax.numpy as jnp
import numpy as np
from jax import lax
from jax.experimental import pallas as pl
from jax.experimental.pallas import tpu as pltpu
from jax.sharding import PartitionSpec as P

MESH = pl.DeviceIdType.MESH
F32 = jnp.float32
BF16 = jnp.bfloat16

M = 64
NLON = 1440
C = 128
X, Y, Z, K = 4, 4, 16, 2
B = Y * K
PLANE = X * B
GROUP = C // X
ROWS = 4
CHUNK = 16


def fourier_table():
    column = np.arange(NLON)
    mode = np.arange(M)
    phase = (mode[:, None] * column[None, :] % NLON) * (2.0 * math.pi / NLON)
    table = np.concatenate([np.cos(phase), -np.sin(phase)], 0) / math.sqrt(NLON)
    return jnp.asarray(table.astype(np.float32), BF16)


def shuffle_table():
    table = np.zeros((ROWS, GROUP, ROWS, ROWS, ROWS, GROUP), np.float32)
    for jj in range(4):
        for c in range(GROUP):
            for a in range(ROWS):
                table[jj, c, a, a, jj, c] = 1
    return jnp.asarray(table.reshape(512, 512), BF16)


def row_table():
    table = np.zeros((Z, X, B, C), np.float32)
    for z in range(Z):
        for b in range(B):
            table[z, :, b, (b // K) * Z * K + z * K + b % K] = 1
    return jnp.asarray(table.reshape(512, C), BF16)


def iota(shape, dim):
    return lax.broadcasted_iota(jnp.int32, shape, dim)


def dot(left, right):
    return jnp.dot(left, right, preferred_element_type=F32)


def dot_t(left, right):
    return lax.dot_general(left, right, (((1,), (1,)), ((), ())), preferred_element_type=F32)


def onehot(mask):
    return jnp.where(mask, 1.0, 0.0).astype(BF16)


def swap_blocks(v):
    lane = iota((8, 128), 1) // 32
    parts = [v[8 * p : 8 * p + 8] for p in range(4)]
    rows = []
    for q in range(4):
        row = parts[q]
        for p in range(4):
            if p != q:
                row = jnp.where(lane == p, pltpu.roll(parts[p], ((p - q) * 32) % 128, 1), row)
        rows.append(row)
    return jnp.concatenate(rows, 0)


def kernel(
    f_hbm, cot_hbm, p_hbm, s_hbm, w_hbm, skip_hbm, tt_hbm, shuffle_hbm, pick_hbm,
    out_hbm, gf_hbm, gw_hbm, gk_hbm,
    f_in, cot_in, p_ref, s_ref, skip_ref, tt_ref, shuffle_ref, pick_ref,
    out_ref, gf_ref, gw_ref, gk_ref,
    fall, gall, wall, act, pbig, sbig, pbig_t, sbig_t, kron1, kron2,
    xs, xr, ys, yr, ms, mr, vs, vr,
    bxs, bxr, bys, byr, bms, bmr, bvs, bvr,
    gws, gwr, k1s, k1r, k2s, k2r, k3r,
    send, recv, local, cot_ref,
):
    lat = lax.axis_index("lat")
    x = lax.axis_index("ch")
    y, z, core = lat // (Z * K), (lat // K) % Z, lat % K
    b = y * K + core
    me = x * B + b

    def plane_device(s):
        bb = s % B
        return ((bb // K) * (Z * K) + z * K + bb % K, s // B)

    def z_device(zz):
        return (y * (Z * K) + zz * K + core, x)

    def remote(src, dst, slot, device):
        return pltpu.make_async_remote_copy(
            src_ref=src, dst_ref=dst, send_sem=send.at[slot], recv_sem=recv.at[slot],
            device_id=device, device_id_type=MESH,
        )

    def to_plane(slot, src, dst):
        @pl.loop(1, PLANE)
        def _(i):
            s = lax.rem(me + i, PLANE)
            remote(src.at[s], dst.at[me], slot, plane_device(s)).start()

        dst[me] = src[me]

    def far(i):
        half = i // 2
        return jnp.where(i % 2 == 0, Z // 2 + half, Z // 2 - half)

    def to_column(slot, src, dst, indexed):
        @pl.loop(1, Z)
        def _(i):
            zz = lax.rem(z + far(i), Z)
            remote(src.at[zz] if indexed else src, dst.at[z], slot, z_device(zz)).start()

        dst[z] = src[z] if indexed else src[...]

    def wait_recv(slot, dst, count):
        part = dst.at[pl.ds(0, count)]
        pltpu.make_async_copy(part, part, recv.at[slot]).wait()

    def wait_send(slot, dst, count):
        part = dst.at[pl.ds(0, count)]
        pltpu.make_async_copy(part, part, send.at[slot]).wait()

    barrier = pltpu.get_barrier_semaphore()

    @pl.loop(1, PLANE)
    def _(i):
        pl.semaphore_signal(
            barrier, inc=1, device_id=plane_device(lax.rem(me + i, PLANE)), device_id_type=MESH
        )

    @pl.loop(1, Z)
    def _(i):
        pl.semaphore_signal(
            barrier, inc=1, device_id=z_device(lax.rem(z + i, Z)), device_id_type=MESH
        )

    def load(src, dst, slot):
        copy = pltpu.make_async_copy(src, dst, local.at[slot])
        copy.start()
        return copy

    loads = [
        load(src, dst, i)
        for i, (src, dst) in enumerate(
            (
                (f_hbm, f_in), (tt_hbm, tt_ref), (shuffle_hbm, shuffle_ref), (p_hbm, p_ref),
                (s_hbm, s_ref), (pick_hbm, pick_ref), (w_hbm.at[0], wall.at[b]),
                (skip_hbm, skip_ref), (cot_hbm, cot_in),
            )
        )
    ]

    def spread(values, dst):
        rounded = values.astype(BF16)
        cat = jnp.concatenate([rounded[32 * jj : 32 * jj + 32] for jj in range(4)], 1)
        for a in range(ROWS):
            dst[:, a, :] = dot(cat, shuffle_ref[:, 128 * a : 128 * a + 128])

    def collect(src):
        cat = jnp.concatenate([src[:, a, :] for a in range(ROWS)], 1).astype(BF16)
        wide = dot_t(cat, shuffle_ref[...])
        tall = jnp.concatenate([wide[:, 128 * jj : 128 * jj + 128] for jj in range(4)], 0)
        return tall.T

    def partial_sums(big, src, dst):
        rows = jnp.concatenate([src[:, a, :] for a in range(ROWS)], 0).astype(BF16)
        dst[...] = dot(big[...], rows).astype(BF16).reshape(Z, 32, 128)

    def total(src):
        acc = src[0].astype(F32)
        for zz in range(1, Z):
            acc = acc + src[zz].astype(F32)
        return swap_blocks(acc)

    def expand_rows(big, src, dst):
        v = dot(big[...], src[...].reshape(512, 128))
        for a in range(ROWS):
            dst[:, a, :] = swap_blocks(v[32 * a : 32 * a + 32])

    def mode_rows(values, mode):
        return jnp.where(iota((32, 128), 0) % 8 == mode, values, 0.0).astype(BF16)

    loads[0].wait()
    fall[x] = f_in[...].reshape(GROUP * ROWS, NLON)
    own = fall.at[x]
    loads[1].wait()
    x_modes = dot_t(tt_ref[...], own[...])
    loads[2].wait()
    spread(x_modes, xs)
    loads[6].wait()
    pl.semaphore_wait(barrier, PLANE - 1 + Z - 1)

    to_plane(0, xs, xr)

    @pl.loop(1, B)
    def _(i):
        bb = lax.rem(b + i, B)
        remote(wall.at[b], wall.at[b], 1, plane_device(x * B + bb)).start()

    def gather_x(slot, ref, half):
        block = ref.at[x, pl.ds(half * 64, 64)]

        @pl.loop(1, X)
        def _(i):
            remote(block, block, slot, (lat, lax.rem(x + i, X))).start()

    def wait_gather(slot, ref):
        part = ref.at[pl.ds(0, X - 1), pl.ds(0, 64)]
        for k in range(2):
            pltpu.make_async_copy(part, part, recv.at[slot + k]).wait()

    def wait_gather_sent(slot, ref):
        part = ref.at[pl.ds(0, X - 1), pl.ds(0, 64)]
        for k in range(2):
            pltpu.make_async_copy(part, part, send.at[slot + k]).wait()

    row = iota((128, 512), 0)
    bb = row % B
    pick_a = onehot(
        iota((128, 512), 1) == (bb // K) * (Z * K * ROWS) + (z * K + bb % K) * ROWS + row // 32
    )
    for i in (3, 4, 5):
        loads[i].wait()
    p_rows = dot_t(pick_a, p_ref[...].astype(BF16)).astype(BF16)
    s_rows = dot(pick_a, s_ref[...].astype(BF16)).astype(BF16)
    same = (iota((512, 128), 0) // 8) % 4 == (iota((512, 128), 1) // 8) % 4
    same_t = (iota((128, 512), 0) // 8) % 4 == (iota((128, 512), 1) // 8) % 4
    pick = pick_ref[...]
    pbig[...] = jnp.where(same, dot_t(pick, p_rows), 0.0).astype(BF16)
    sbig[...] = jnp.where(same_t, dot_t(s_rows, pick), 0.0).astype(BF16)
    sbig_t[...] = jnp.where(same, dot_t(pick, s_rows), 0.0).astype(BF16)
    pbig_t[...] = jnp.where(same_t, dot_t(p_rows, pick), 0.0).astype(BF16)

    wait_recv(0, xr, PLANE - 1)
    partial_sums(pbig, xr, ys)
    to_column(3, ys, yr, True)
    gather_x(15, fall, 0)

    loads[7].wait()
    pick_g = onehot(iota((128, 128), 1) == x * GROUP + iota((128, 128), 0) // ROWS)
    each = onehot(iota((128, 512), 0) == iota((128, 512), 1) // ROWS)
    same_row = iota((128, 512), 0) % ROWS == iota((128, 512), 1) % ROWS
    skip = skip_ref[...]
    kron1[...] = jnp.where(same_row, dot(dot_t(pick_g, skip).astype(BF16), each), 0.0).astype(BF16)
    kron2[...] = jnp.where(same_row, dot(dot(pick_g, skip).astype(BF16), each), 0.0).astype(BF16)

    loads[8].wait()
    cot_ref[...] = cot_in[...].reshape(GROUP * ROWS, NLON)

    wait_recv(1, wall, B - 1)
    wait_recv(3, yr, Z - 1)
    spectral = total(yr).astype(BF16).astype(F32)
    w0 = wall[:, 0].reshape(B * C, C)
    w1 = wall[:, 1].reshape(B * C, C)
    wide = jnp.concatenate([mode_rows(spectral, m) for m in range(B)], 1)
    r0, r1 = dot(wide, w0), dot(wide, w1)
    mixed = jnp.concatenate([r0[:16] - r1[16:], r0[16:] + r1[:16]], 0)
    ms[...] = mixed.astype(BF16)
    to_column(4, ms, mr, False)
    gather_x(16, fall, 1)
    for jj in range(4):
        gws[:, jj, :] = spectral[8 * jj : 8 * jj + 8]

    wait_recv(4, mr, Z - 1)
    expand_rows(sbig, mr, vs)
    to_plane(5, vs, vr)

    wait_gather(15, fall)
    acc = dot(kron1[:, 0:128], fall[0])
    for g in range(1, X):
        acc = acc + dot(kron1[:, 128 * g : 128 * g + 128], fall[g])
    act[...] = acc

    col = iota((128, 128), 1) % M
    doubling = jnp.where(col == 0, 1.0, 2.0)
    wait_recv(5, vr, PLANE - 1)
    v_modes = (collect(vr) * doubling).astype(BF16)
    act[...] += dot(v_modes, tt_ref[...])

    scale = math.sqrt(2.0 / math.pi)

    g_ref = gall.at[x]

    @pl.loop(0, 128 // CHUNK)
    def _(i):
        rows = pl.ds(pl.multiple_of(i * CHUNK, CHUNK), CHUNK)
        u = act[rows, :]
        square = u * u
        t = jnp.tanh(scale * u * (1.0 + 0.044715 * square))
        cdf = 0.5 * (1.0 + t)
        out_ref[rows, :] = (u * cdf).astype(BF16)
        slope = cdf + 0.5 * u * (1.0 - t * t) * (scale * (1.0 + 3 * 0.044715 * square))
        g_ref[rows, :] = (cot_ref[rows, :].astype(F32) * slope).astype(BF16)

    g_pre = g_ref[...]
    row = iota((128, 128), 0) % M
    doubling_t = jnp.where(row == 0, 1.0, 2.0)
    spread(dot_t(tt_ref[...], g_pre) * doubling_t, bxs)
    to_plane(6, bxs, bxr)

    f_in[...] = out_ref[...].reshape(GROUP, ROWS, NLON)
    store_out = load(f_in, out_hbm, 0)

    same_lane = iota((128, 128), 0) % ROWS == iota((128, 128), 1) % ROWS
    term = jnp.zeros((128, 128), F32)
    for g in range(X):
        full = jnp.where(same_lane, dot_t(g_pre, fall[g]), 0.0)
        lanes = jnp.where(iota((128, 128), 1) == GROUP * g + iota((128, 128), 0) // ROWS, 1.0, 0.0)
        term = term + jnp.dot(
            full, lanes, precision=lax.Precision.HIGHEST, preferred_element_type=F32
        )
    fold = jnp.where(iota((32, 128), 0) == iota((32, 128), 1) // ROWS, 1.0, 0.0)
    term = jnp.dot(fold, term, precision=lax.Precision.HIGHEST, preferred_element_type=F32)
    for i in range(ROWS):
        k1s[:, i, :] = term[8 * i : 8 * i + 8]

    @pl.loop(1, B)
    def _(i):
        bb = lax.rem(b + i, B)
        remote(k1s.at[bb], k1r.at[b], 9, plane_device(x * B + bb)).start()

    k1r[b] = k1s[b]

    wait_recv(6, bxr, PLANE - 1)
    partial_sums(sbig_t, bxr, bys)
    to_column(8, bys, byr, True)
    gather_x(17, gall, 0)

    wait_recv(9, k1r, B - 1)
    acc = k1r[0]
    for i in range(1, B):
        acc = acc + k1r[i]
    k2s[...] = acc

    wait_recv(8, byr, Z - 1)
    g_mixed = total(byr).astype(BF16).astype(F32)
    r0 = jnp.zeros((32, C), F32)
    r1 = jnp.zeros((32, C), F32)
    for m in range(B):
        masked = mode_rows(g_mixed, m)
        r0 = r0 + dot_t(masked, wall[m, 0])
        r1 = r1 + dot_t(masked, wall[m, 1])
    g_spectral = jnp.concatenate([r0[:16] + r1[16:], r0[16:] - r1[:16]], 0)
    bms[...] = g_spectral.astype(BF16)
    to_column(10, bms, bmr, False)

    @pl.loop(1, Z)
    def _(i):
        zz = lax.rem(z + far(i), Z)
        remote(k2s, k2r.at[z], 12, z_device(zz)).start()

    k2r[z] = k2s[...]

    for jj in range(4):
        gws[:, 4 + jj, :] = g_mixed[8 * jj : 8 * jj + 8]

    @pl.loop(1, PLANE)
    def _(i):
        s = lax.rem(me + i, PLANE)
        remote(gws.at[s % B], gwr.at[me], 11, plane_device(s)).start()

    gwr[me] = gws[b]
    gather_x(18, gall, 1)

    wait_recv(11, gwr, PLANE - 1)
    s_all = jnp.concatenate([gwr[:, jj, :] for jj in range(4)], 0).astype(BF16)
    g_all = jnp.concatenate([gwr[:, 4 + jj, :] for jj in range(4)], 0).astype(BF16)
    pick_o = onehot(iota((GROUP, 128), 1) == x * GROUP + iota((GROUP, 128), 0))
    g_own = dot_t(pick_o, g_all)
    g_turn = jnp.concatenate([g_own[:, 64:], -g_own[:, :64]], 1)
    gw_ref[0] = dot(g_own.astype(BF16), s_all) * (1.0 / math.sqrt(2 * M))
    gw_ref[1] = dot(g_turn.astype(BF16), s_all) * (1.0 / math.sqrt(2 * M))
    store_gw = load(gw_ref, gw_hbm, 1)

    wait_recv(10, bmr, Z - 1)
    expand_rows(pbig_t, bmr, bvs)
    to_plane(13, bvs, bvr)

    wait_recv(12, k2r, Z - 1)
    acc = k2r[0]
    for i in range(1, Z):
        acc = acc + k2r[i]
    k3r[b] = acc * (1.0 / math.sqrt(Y * Z * K * ROWS * NLON))

    @pl.loop(1, B)
    def _(i):
        bb = lax.rem(b + i, B)
        remote(k3r.at[b], k3r.at[b], 14, plane_device(x * B + bb)).start()

    wait_gather(17, gall)
    acc = dot(kron2[:, 0:128], gall[0])
    for g in range(1, X):
        acc = acc + dot(kron2[:, 128 * g : 128 * g + 128], gall[g])
    act[...] = acc

    wait_recv(14, k3r, B - 1)
    gk_ref[...] = jnp.concatenate([k3r[:, i, :] for i in range(ROWS)], 0)
    store_gk = load(gk_ref, gk_hbm, 2)

    wait_recv(13, bvr, PLANE - 1)
    result = act[...] + dot(collect(bvr).astype(BF16), tt_ref[...])
    gf_ref[...] = result.reshape(GROUP, ROWS, NLON).astype(BF16)
    store_gf = load(gf_ref, gf_hbm, 3)

    wait_send(0, xs, PLANE - 1)
    wait_send(1, wall, B - 1)
    wait_gather_sent(15, fall)
    wait_send(3, ys, Z - 1)
    wait_send(4, mr, Z - 1)
    wait_send(5, vs, PLANE - 1)
    wait_send(6, bxs, PLANE - 1)
    wait_gather_sent(17, gall)
    wait_send(8, bys, Z - 1)
    wait_send(9, k1s, B - 1)
    wait_send(10, bmr, Z - 1)
    wait_send(11, gwr, PLANE - 1)
    wait_send(12, k2r, Z - 1)
    wait_send(13, bvs, PLANE - 1)
    wait_send(14, k3r, B - 1)
    for copy in (store_out, store_gw, store_gk, store_gf):
        copy.wait()


def on_device(features, projection, synthesis, mode_weights, skip_weights, cotangent):
    anywhere = pl.BlockSpec(memory_space=pl.ANY)
    plane = pltpu.VMEM((PLANE, ROWS, 128), F32)
    column = pltpu.VMEM((Z, 32, 128), BF16)
    one = pltpu.VMEM((32, 128), BF16)
    tall = pltpu.VMEM((512, 128), BF16)
    flat = pltpu.VMEM((128, 512), BF16)
    field = pltpu.VMEM((X, GROUP * ROWS, NLON), BF16)
    phases = [plane, plane, column, column, one, column, plane, plane]
    out, grad_features, grad_weights, grad_skip = pl.pallas_call(
        kernel,
        out_shape=(
            jax.ShapeDtypeStruct((GROUP, ROWS, NLON), BF16),
            jax.ShapeDtypeStruct((GROUP, ROWS, NLON), BF16),
            jax.ShapeDtypeStruct((2, GROUP, C), F32),
            jax.ShapeDtypeStruct((GROUP, C), F32),
        ),
        in_specs=[anywhere] * 9,
        out_specs=[anywhere] * 4,
        scratch_shapes=[
            pltpu.VMEM((GROUP, ROWS, NLON), BF16),
            pltpu.VMEM((GROUP, ROWS, NLON), BF16),
            pltpu.VMEM((C, 512), F32),
            pltpu.VMEM((512, C), F32),
            pltpu.VMEM((C, C), BF16),
            pltpu.VMEM((C, NLON), BF16),
            pltpu.VMEM((512, 512), BF16),
            pltpu.VMEM((512, C), BF16),
            pltpu.VMEM((GROUP * ROWS, NLON), BF16),
            pltpu.VMEM((GROUP, ROWS, NLON), BF16),
            pltpu.VMEM((2, GROUP, C), F32),
            pltpu.VMEM((GROUP, C), F32),
            field,
            field,
            pltpu.VMEM((B, 2, C, C), BF16),
            pltpu.VMEM((GROUP * ROWS, NLON), F32),
            tall, flat, flat, tall, flat, flat,
            *phases,
            *phases,
            pltpu.VMEM((B, 8, 128), F32),
            pltpu.VMEM((PLANE, 8, 128), F32),
            pltpu.VMEM((B, ROWS, 128), F32),
            pltpu.VMEM((B, ROWS, 128), F32),
            pltpu.VMEM((ROWS, 128), F32),
            pltpu.VMEM((Z, ROWS, 128), F32),
            pltpu.VMEM((B, ROWS, 128), F32),
            pltpu.SemaphoreType.DMA((19,)),
            pltpu.SemaphoreType.DMA((19,)),
            pltpu.SemaphoreType.DMA((9,)),
            pltpu.VMEM((GROUP * ROWS, NLON), BF16),
        ],
        compiler_params=pltpu.CompilerParams(
            collective_id=0, has_side_effects=True, vmem_limit_bytes=56 * 1024 * 1024
        ),
    )(
        features,
        cotangent,
        projection,
        synthesis,
        mode_weights,
        skip_weights,
        fourier_table(),
        shuffle_table(),
        row_table(),
    )
    return (out, grad_features, grad_weights.transpose(0, 2, 1)[None], grad_skip.T)


def solution(mesh):
    placed = (P("ch", "lat", None), P(), P(), P("lat", None, None, None), P(), P("ch", "lat", None))
    return jax.shard_map(
        on_device,
        mesh=mesh,
        in_specs=placed,
        out_specs=(
            P("ch", "lat", None),
            P("ch", "lat", None),
            P("lat", None, None, "ch"),
            P(None, "ch"),
        ),
        check_vma=False,
    )
```

```python
import math

import jax
import jax.numpy as jnp
import numpy as np
from jax import lax
from jax.experimental import pallas as pl
from jax.experimental.pallas import tpu as pltpu
from jax.sharding import PartitionSpec as P

MESH = pl.DeviceIdType.MESH
F32 = jnp.float32
BF16 = jnp.bfloat16

M = 64
NLON = 1440
C = 128
X, Y, Z, K = 4, 4, 16, 2
B = Y * K
PLANE = X * B
GROUP = C // X
ROWS = 4
CHUNK = 16


def fourier_table():
    column = np.arange(NLON)
    mode = np.arange(M)
    phase = (mode[:, None] * column[None, :] % NLON) * (2.0 * math.pi / NLON)
    table = np.concatenate([np.cos(phase), -np.sin(phase)], 0) / math.sqrt(NLON)
    return jnp.asarray(table.astype(np.float32), BF16)


def shuffle_table():
    table = np.zeros((ROWS, GROUP, ROWS, ROWS, ROWS, GROUP), np.float32)
    for jj in range(4):
        for c in range(GROUP):
            for a in range(ROWS):
                table[jj, c, a, a, jj, c] = 1
    return jnp.asarray(table.reshape(512, 512), BF16)


def row_table():
    table = np.zeros((Z, X, B, C), np.float32)
    for z in range(Z):
        for b in range(B):
            table[z, :, b, (b // K) * Z * K + z * K + b % K] = 1
    return jnp.asarray(table.reshape(512, C), BF16)


def iota(shape, dim):
    return lax.broadcasted_iota(jnp.int32, shape, dim)


def dot(left, right):
    return jnp.dot(left, right, preferred_element_type=F32)


def dot_t(left, right):
    return lax.dot_general(left, right, (((1,), (1,)), ((), ())), preferred_element_type=F32)


def onehot(mask):
    return jnp.where(mask, 1.0, 0.0).astype(BF16)


def swap_blocks(v):
    lane = iota((8, 128), 1) // 32
    parts = [v[8 * p : 8 * p + 8] for p in range(4)]
    rows = []
    for q in range(4):
        row = parts[q]
        for p in range(4):
            if p != q:
                row = jnp.where(lane == p, pltpu.roll(parts[p], ((p - q) * 32) % 128, 1), row)
        rows.append(row)
    return jnp.concatenate(rows, 0)


def kernel(
    f_hbm, cot_hbm, p_hbm, s_hbm, w_hbm, skip_hbm, tt_hbm, shuffle_hbm, pick_hbm,
    out_hbm, gf_hbm, gw_hbm, gk_hbm,
    f_in, cot_in, p_ref, s_ref, skip_ref, tt_ref, shuffle_ref, pick_ref,
    out_ref, gf_ref, gw_ref, gk_ref,
    fall, gall, wall, act, pbig, sbig, pbig_t, sbig_t, kron1, kron2,
    xs, xr, ys, yr, ms, mr, vs, vr,
    bxs, bxr, bys, byr, bms, bmr, bvs, bvr,
    gws, gwr, k1s, k1r, k2s, k2r, k3r,
    send, recv, local, cot_ref, wall_t,
):
    lat = lax.axis_index("lat")
    x = lax.axis_index("ch")
    y, z, core = lat // (Z * K), (lat // K) % Z, lat % K
    b = y * K + core
    me = x * B + b

    def plane_device(s):
        bb = s % B
        return ((bb // K) * (Z * K) + z * K + bb % K, s // B)

    def z_device(zz):
        return (y * (Z * K) + zz * K + core, x)

    def remote(src, dst, slot, device):
        return pltpu.make_async_remote_copy(
            src_ref=src, dst_ref=dst, send_sem=send.at[slot], recv_sem=recv.at[slot],
            device_id=device, device_id_type=MESH,
        )

    def peer(i):
        def ring(k):
            return jnp.where(k == 3, 0, jnp.where(k == 2, 3, 2 - k))

        dx, dy, dc = ring(i // B), ring((i // K) % Y), 1 - i % K
        return ((x + dx) % X) * B + ((y + dy) % Y) * K + (core + dc) % K

    def to_plane(slot, src, dst):
        @pl.loop(0, PLANE - 1, unroll=True)
        def _(i):
            s = peer(i)
            remote(src.at[s], dst.at[me], slot, plane_device(s)).start()

        dst[me] = src[me]

    def far(i):
        half = i // 2
        return jnp.where(i % 2 == 0, Z // 2 + half, Z // 2 - half)

    def to_column(slot, src, dst, indexed):
        @pl.loop(1, Z, unroll=True)
        def _(i):
            zz = lax.rem(z + far(i), Z)
            remote(src.at[zz] if indexed else src, dst.at[z], slot, z_device(zz)).start()

        dst[z] = src[z] if indexed else src[...]

    def wait_recv(slot, dst, count):
        part = dst.at[pl.ds(0, count)]
        pltpu.make_async_copy(part, part, recv.at[slot]).wait()

    def wait_send(slot, dst, count):
        part = dst.at[pl.ds(0, count)]
        pltpu.make_async_copy(part, part, send.at[slot]).wait()

    barrier = pltpu.get_barrier_semaphore()

    @pl.loop(1, Z, unroll=True)
    def _(i):
        pl.semaphore_signal(
            barrier, inc=1, device_id=z_device(lax.rem(z + far(i), Z)), device_id_type=MESH
        )

    @pl.loop(0, PLANE - 1, unroll=True)
    def _(i):
        pl.semaphore_signal(
            barrier, inc=1, device_id=plane_device(peer(i)), device_id_type=MESH
        )

    def load(src, dst, slot):
        copy = pltpu.make_async_copy(src, dst, local.at[slot])
        copy.start()
        return copy

    loads = [
        load(src, dst, i)
        for i, (src, dst) in enumerate(
            (
                (f_hbm, f_in), (tt_hbm, tt_ref), (shuffle_hbm, shuffle_ref), (p_hbm, p_ref),
                (s_hbm, s_ref), (pick_hbm, pick_ref), (w_hbm.at[0], wall.at[b]),
                (skip_hbm, skip_ref), (cot_hbm, cot_in),
            )
        )
    ]

    def spread(values, dst):
        rounded = values.astype(BF16)
        cat = jnp.concatenate([rounded[32 * jj : 32 * jj + 32] for jj in range(4)], 1)
        for a in range(ROWS):
            dst[:, a, :] = dot(cat, shuffle_ref[:, 128 * a : 128 * a + 128])

    def collect(src):
        cat = jnp.concatenate([src[:, a, :] for a in range(ROWS)], 1).astype(BF16)
        wide = dot_t(cat, shuffle_ref[...])
        tall = jnp.concatenate([wide[:, 128 * jj : 128 * jj + 128] for jj in range(4)], 0)
        return tall.T

    def partial_sums(big, src, dst):
        rows = jnp.concatenate([src[:, a, :] for a in range(ROWS)], 0).astype(BF16)
        dst[...] = dot(big[...], rows).astype(BF16).reshape(Z, 32, 128)

    def total(src):
        acc = src[0].astype(F32)
        for zz in range(1, Z):
            acc = acc + src[zz].astype(F32)
        return swap_blocks(acc)

    def expand_rows(big, src, dst):
        v = dot(big[...], src[...].reshape(512, 128))
        for a in range(ROWS):
            dst[:, a, :] = swap_blocks(v[32 * a : 32 * a + 32])

    def mode_rows(values, mode):
        return jnp.where(iota((32, 128), 0) % 8 == mode, values, 0.0).astype(BF16)

    loads[0].wait()
    fall[x] = f_in[...].reshape(GROUP * ROWS, NLON)
    own = fall.at[x]
    loads[1].wait()
    x_modes = dot_t(tt_ref[...], own[...])
    loads[2].wait()
    spread(x_modes, xs)
    loads[6].wait()
    pl.semaphore_wait(barrier, PLANE - 1 + Z - 1)

    to_plane(0, xs, xr)

    @pl.loop(1, B)
    def _(i):
        bb = lax.rem(b + i, B)
        remote(wall.at[b], wall.at[b], 1, plane_device(x * B + bb)).start()

    def gather_x(slot, ref, half):
        block = ref.at[x, pl.ds(half * 64, 64)]

        @pl.loop(1, X)
        def _(i):
            remote(block, block, slot, (lat, lax.rem(x + i, X))).start()

    def wait_gather(slot, ref):
        part = ref.at[pl.ds(0, X - 1), pl.ds(0, 64)]
        for k in range(2):
            pltpu.make_async_copy(part, part, recv.at[slot + k]).wait()

    def wait_gather_sent(slot, ref):
        part = ref.at[pl.ds(0, X - 1), pl.ds(0, 64)]
        for k in range(2):
            pltpu.make_async_copy(part, part, send.at[slot + k]).wait()

    row = iota((128, 512), 0)
    bb = row % B
    pick_a = onehot(
        iota((128, 512), 1) == (bb // K) * (Z * K * ROWS) + (z * K + bb % K) * ROWS + row // 32
    )
    for i in (3, 4, 5):
        loads[i].wait()
    p_rows = dot_t(pick_a, p_ref[...].astype(BF16)).astype(BF16)
    s_rows = dot(pick_a, s_ref[...].astype(BF16)).astype(BF16)
    same = (iota((512, 128), 0) // 8) % 4 == (iota((512, 128), 1) // 8) % 4
    same_t = (iota((128, 512), 0) // 8) % 4 == (iota((128, 512), 1) // 8) % 4
    pick = pick_ref[...]
    pbig[...] = jnp.where(same, dot_t(pick, p_rows), 0.0).astype(BF16)
    sbig[...] = jnp.where(same_t, dot_t(s_rows, pick), 0.0).astype(BF16)
    sbig_t[...] = jnp.where(same, dot_t(pick, s_rows), 0.0).astype(BF16)
    pbig_t[...] = jnp.where(same_t, dot_t(p_rows, pick), 0.0).astype(BF16)

    wait_recv(0, xr, PLANE - 1)
    partial_sums(pbig, xr, ys)
    to_column(3, ys, yr, True)
    gather_x(15, fall, 0)

    loads[7].wait()
    pick_g = onehot(iota((128, 128), 1) == x * GROUP + iota((128, 128), 0) // ROWS)
    each = onehot(iota((128, 512), 0) == iota((128, 512), 1) // ROWS)
    same_row = iota((128, 512), 0) % ROWS == iota((128, 512), 1) % ROWS
    skip = skip_ref[...]
    kron1[...] = jnp.where(same_row, dot(dot_t(pick_g, skip).astype(BF16), each), 0.0).astype(BF16)
    kron2[...] = jnp.where(same_row, dot(dot(pick_g, skip).astype(BF16), each), 0.0).astype(BF16)

    loads[8].wait()
    cot_ref[...] = cot_in[...].reshape(GROUP * ROWS, NLON)

    wait_recv(1, wall, B - 1)
    wait_recv(3, yr, Z - 1)
    spectral = total(yr).astype(BF16).astype(F32)
    w0 = wall[:, 0].reshape(B * C, C)
    w1 = wall[:, 1].reshape(B * C, C)
    wide = jnp.concatenate([mode_rows(spectral, m) for m in range(B)], 1)
    r0, r1 = dot(wide, w0), dot(wide, w1)
    mixed = jnp.concatenate([r0[:16] - r1[16:], r0[16:] + r1[:16]], 0)
    ms[...] = mixed.astype(BF16)
    to_column(4, ms, mr, False)
    gather_x(16, fall, 1)
    for jj in range(4):
        gws[:, jj, :] = spectral[8 * jj : 8 * jj + 8]

    for m in range(B):
        for part in range(2):
            wall_t[part, 128 * m : 128 * m + 128] = wall[m, part].T

    wait_recv(4, mr, Z - 1)
    expand_rows(sbig, mr, vs)
    to_plane(5, vs, vr)

    wait_gather(15, fall)
    acc = dot(kron1[:, 0:128], fall[0])
    for g in range(1, X):
        acc = acc + dot(kron1[:, 128 * g : 128 * g + 128], fall[g])
    act[...] = acc

    col = iota((128, 128), 1) % M
    doubling = jnp.where(col == 0, 1.0, 2.0)
    wait_recv(5, vr, PLANE - 1)
    v_modes = (collect(vr) * doubling).astype(BF16)
    act[...] += dot(v_modes, tt_ref[...])

    scale = math.sqrt(2.0 / math.pi)

    g_ref = gall.at[x]

    @pl.loop(0, 128 // CHUNK)
    def _(i):
        rows = pl.ds(pl.multiple_of(i * CHUNK, CHUNK), CHUNK)
        u = act[rows, :]
        square = u * u
        t = jnp.tanh(scale * u * (1.0 + 0.044715 * square))
        cdf = 0.5 * (1.0 + t)
        out_ref[rows, :] = (u * cdf).astype(BF16)
        slope = cdf + 0.5 * u * (1.0 - t * t) * (scale * (1.0 + 3 * 0.044715 * square))
        g_ref[rows, :] = (cot_ref[rows, :].astype(F32) * slope).astype(BF16)

    g_pre = g_ref[...]
    row = iota((128, 128), 0) % M
    doubling_t = jnp.where(row == 0, 1.0, 2.0)
    spread(dot_t(tt_ref[...], g_pre) * doubling_t, bxs)
    to_plane(6, bxs, bxr)

    f_in[...] = out_ref[...].reshape(GROUP, ROWS, NLON)
    store_out = load(f_in, out_hbm, 0)

    same_lane = iota((128, 128), 0) % ROWS == iota((128, 128), 1) % ROWS
    term = jnp.zeros((128, 128), F32)
    for g in range(X):
        full = jnp.where(same_lane, dot_t(g_pre, fall[g]), 0.0)
        lanes = jnp.where(iota((128, 128), 1) == GROUP * g + iota((128, 128), 0) // ROWS, 1.0, 0.0)
        term = term + jnp.dot(
            full, lanes, precision=lax.Precision.HIGHEST, preferred_element_type=F32
        )
    fold = jnp.where(iota((32, 128), 0) == iota((32, 128), 1) // ROWS, 1.0, 0.0)
    term = jnp.dot(fold, term, precision=lax.Precision.HIGHEST, preferred_element_type=F32)
    for i in range(ROWS):
        k1s[:, i, :] = term[8 * i : 8 * i + 8]

    @pl.loop(1, B)
    def _(i):
        bb = lax.rem(b + i, B)
        remote(k1s.at[bb], k1r.at[b], 9, plane_device(x * B + bb)).start()

    k1r[b] = k1s[b]

    wait_recv(6, bxr, PLANE - 1)
    partial_sums(sbig_t, bxr, bys)
    to_column(8, bys, byr, True)
    gather_x(17, gall, 0)

    wait_recv(9, k1r, B - 1)
    acc = k1r[0]
    for i in range(1, B):
        acc = acc + k1r[i]
    k2s[...] = acc

    wait_recv(8, byr, Z - 1)
    g_mixed = total(byr).astype(BF16).astype(F32)
    wide = jnp.concatenate([mode_rows(g_mixed, m) for m in range(B)], 1)
    r0, r1 = dot(wide, wall_t[0]), dot(wide, wall_t[1])
    g_spectral = jnp.concatenate([r0[:16] + r1[16:], r0[16:] - r1[:16]], 0)
    bms[...] = g_spectral.astype(BF16)
    to_column(10, bms, bmr, False)

    @pl.loop(1, Z, unroll=True)
    def _(i):
        zz = lax.rem(z + far(i), Z)
        remote(k2s, k2r.at[z], 12, z_device(zz)).start()

    k2r[z] = k2s[...]

    for jj in range(4):
        gws[:, 4 + jj, :] = g_mixed[8 * jj : 8 * jj + 8]

    @pl.loop(1, PLANE)
    def _(i):
        s = lax.rem(me + i, PLANE)
        remote(gws.at[s % B], gwr.at[me], 11, plane_device(s)).start()

    gwr[me] = gws[b]
    gather_x(18, gall, 1)

    wait_recv(11, gwr, PLANE - 1)
    s_all = jnp.concatenate([gwr[:, jj, :] for jj in range(4)], 0).astype(BF16)
    g_all = jnp.concatenate([gwr[:, 4 + jj, :] for jj in range(4)], 0).astype(BF16)
    pick_o = onehot(iota((GROUP, 128), 1) == x * GROUP + iota((GROUP, 128), 0))
    g_own = dot_t(pick_o, g_all)
    g_turn = jnp.concatenate([g_own[:, 64:], -g_own[:, :64]], 1)
    gw_ref[0] = dot(g_own.astype(BF16), s_all) * (1.0 / math.sqrt(2 * M))
    gw_ref[1] = dot(g_turn.astype(BF16), s_all) * (1.0 / math.sqrt(2 * M))
    store_gw = load(gw_ref, gw_hbm, 1)

    wait_recv(10, bmr, Z - 1)
    expand_rows(pbig_t, bmr, bvs)
    to_plane(13, bvs, bvr)

    wait_recv(12, k2r, Z - 1)
    acc = k2r[0]
    for i in range(1, Z):
        acc = acc + k2r[i]
    k3r[b] = acc * (1.0 / math.sqrt(Y * Z * K * ROWS * NLON))

    @pl.loop(1, B)
    def _(i):
        bb = lax.rem(b + i, B)
        remote(k3r.at[b], k3r.at[b], 14, plane_device(x * B + bb)).start()

    wait_gather(17, gall)
    acc = dot(kron2[:, 0:128], gall[0])
    for g in range(1, X):
        acc = acc + dot(kron2[:, 128 * g : 128 * g + 128], gall[g])
    act[...] = acc

    wait_recv(14, k3r, B - 1)
    gk_ref[...] = jnp.concatenate([k3r[:, i, :] for i in range(ROWS)], 0)
    store_gk = load(gk_ref, gk_hbm, 2)

    wait_recv(13, bvr, PLANE - 1)
    result = act[...] + dot(collect(bvr).astype(BF16), tt_ref[...])
    gf_ref[...] = result.reshape(GROUP, ROWS, NLON).astype(BF16)
    store_gf = load(gf_ref, gf_hbm, 3)

    wait_send(0, xs, PLANE - 1)
    wait_send(1, wall, B - 1)
    wait_gather_sent(15, fall)
    wait_send(3, ys, Z - 1)
    wait_send(4, mr, Z - 1)
    wait_send(5, vs, PLANE - 1)
    wait_send(6, bxs, PLANE - 1)
    wait_gather_sent(17, gall)
    wait_send(8, bys, Z - 1)
    wait_send(9, k1s, B - 1)
    wait_send(10, bmr, Z - 1)
    wait_send(11, gwr, PLANE - 1)
    wait_send(12, k2r, Z - 1)
    wait_send(13, bvs, PLANE - 1)
    wait_send(14, k3r, B - 1)
    for copy in (store_out, store_gw, store_gk, store_gf):
        copy.wait()


def copy_out(*refs):
    sources, targets, held = refs[:4], refs[4:8], refs[8:12]
    loaded, stored = refs[12:]
    loads = [pltpu.make_async_copy(sources[i], held[i], loaded.at[i]) for i in range(4)]
    stores = [pltpu.make_async_copy(held[i], targets[i], stored.at[i]) for i in range(4)]
    for load in loads:
        load.start()
    for load, store in zip(loads, stores):
        load.wait()
        store.start()
    for store in stores:
        store.wait()


def on_device(features, projection, synthesis, mode_weights, skip_weights, cotangent):
    anywhere = pl.BlockSpec(memory_space=pl.ANY)
    plane = pltpu.VMEM((PLANE, ROWS, 128), F32)
    column = pltpu.VMEM((Z, 32, 128), BF16)
    one = pltpu.VMEM((32, 128), BF16)
    tall = pltpu.VMEM((512, 128), BF16)
    flat = pltpu.VMEM((128, 512), BF16)
    field = pltpu.VMEM((X, GROUP * ROWS, NLON), BF16)
    phases = [plane, plane, column, column, one, column, plane, plane]
    results = (
        jax.ShapeDtypeStruct((GROUP, ROWS, NLON), BF16),
        jax.ShapeDtypeStruct((GROUP, ROWS, NLON), BF16),
        jax.ShapeDtypeStruct((2, GROUP, C), F32),
        jax.ShapeDtypeStruct((GROUP, C), F32),
    )
    kept = pl.pallas_call(
        kernel,
        out_shape=results,
        in_specs=[anywhere] * 9,
        out_specs=[anywhere] * 4,
        scratch_shapes=[
            pltpu.VMEM((GROUP, ROWS, NLON), BF16),
            pltpu.VMEM((GROUP, ROWS, NLON), BF16),
            pltpu.VMEM((C, 512), F32),
            pltpu.VMEM((512, C), F32),
            pltpu.VMEM((C, C), BF16),
            pltpu.VMEM((C, NLON), BF16),
            pltpu.VMEM((512, 512), BF16),
            pltpu.VMEM((512, C), BF16),
            pltpu.VMEM((GROUP * ROWS, NLON), BF16),
            pltpu.VMEM((GROUP, ROWS, NLON), BF16),
            pltpu.VMEM((2, GROUP, C), F32),
            pltpu.VMEM((GROUP, C), F32),
            field,
            field,
            pltpu.VMEM((B, 2, C, C), BF16),
            pltpu.VMEM((GROUP * ROWS, NLON), F32),
            tall, flat, flat, tall, flat, flat,
            *phases,
            *phases,
            pltpu.VMEM((B, 8, 128), F32),
            pltpu.VMEM((PLANE, 8, 128), F32),
            pltpu.VMEM((B, ROWS, 128), F32),
            pltpu.VMEM((B, ROWS, 128), F32),
            pltpu.VMEM((ROWS, 128), F32),
            pltpu.VMEM((Z, ROWS, 128), F32),
            pltpu.VMEM((B, ROWS, 128), F32),
            pltpu.SemaphoreType.DMA((19,)),
            pltpu.SemaphoreType.DMA((19,)),
            pltpu.SemaphoreType.DMA((9,)),
            pltpu.VMEM((GROUP * ROWS, NLON), BF16),
            pltpu.VMEM((2, B * C, C), BF16),
        ],
        compiler_params=pltpu.CompilerParams(
            collective_id=0, has_side_effects=True, vmem_limit_bytes=56 * 1024 * 1024
        ),
    )(
        features,
        cotangent,
        projection,
        synthesis,
        mode_weights,
        skip_weights,
        fourier_table(),
        shuffle_table(),
        row_table(),
    )
    out, grad_features, grad_weights, grad_skip = pl.pallas_call(
        copy_out,
        out_shape=results,
        in_specs=[anywhere] * 4,
        out_specs=[anywhere] * 4,
        scratch_shapes=[
            *[pltpu.VMEM(r.shape, r.dtype) for r in results],
            pltpu.SemaphoreType.DMA((4,)),
            pltpu.SemaphoreType.DMA((4,)),
        ],
        compiler_params=pltpu.CompilerParams(vmem_limit_bytes=56 * 1024 * 1024),
        name="copy_out",
    )(*kept)
    return (out, grad_features, grad_weights.transpose(0, 2, 1)[None], grad_skip.T)


def solution(mesh):
    placed = (P("ch", "lat", None), P(), P(), P("lat", None, None, None), P(), P("ch", "lat", None))
    return jax.shard_map(
        on_device,
        mesh=mesh,
        in_specs=placed,
        out_specs=(
            P("ch", "lat", None),
            P("ch", "lat", None),
            P("lat", None, None, "ch"),
            P(None, "ch"),
        ),
        check_vma=False,
    )
```

```python
import math

import jax
import jax.numpy as jnp
import numpy as np
from jax import lax
from jax.experimental import pallas as pl
from jax.experimental.pallas import tpu as pltpu
from jax.sharding import PartitionSpec as P

MESH = pl.DeviceIdType.MESH
F32 = jnp.float32
BF16 = jnp.bfloat16

M = 64
NLON = 1440
C = 128
X, Y, Z, K = 4, 4, 16, 2
B = Y * K
PLANE = X * B
GROUP = C // X
ROWS = 4
CHUNK = 16


def fourier_table():
    column = np.arange(NLON)
    mode = np.arange(M)
    phase = (mode[:, None] * column[None, :] % NLON) * (2.0 * math.pi / NLON)
    table = np.concatenate([np.cos(phase), -np.sin(phase)], 0) / math.sqrt(NLON)
    return jnp.asarray(table.astype(np.float32), BF16)


def shuffle_table():
    table = np.zeros((ROWS, GROUP, ROWS, ROWS, ROWS, GROUP), np.float32)
    for jj in range(4):
        for c in range(GROUP):
            for a in range(ROWS):
                table[jj, c, a, a, jj, c] = 1
    return jnp.asarray(table.reshape(512, 512), BF16)


def row_table():
    table = np.zeros((Z, X, B, C), np.float32)
    for z in range(Z):
        for b in range(B):
            table[z, :, b, (b // K) * Z * K + z * K + b % K] = 1
    return jnp.asarray(table.reshape(512, C), BF16)


def iota(shape, dim):
    return lax.broadcasted_iota(jnp.int32, shape, dim)


def dot(left, right):
    return jnp.dot(left, right, preferred_element_type=F32)


def dot_t(left, right):
    return lax.dot_general(left, right, (((1,), (1,)), ((), ())), preferred_element_type=F32)


def onehot(mask):
    return jnp.where(mask, 1.0, 0.0).astype(BF16)


def swap_blocks(v):
    lane = iota((8, 128), 1) // 32
    parts = [v[8 * p : 8 * p + 8] for p in range(4)]
    rows = []
    for q in range(4):
        row = parts[q]
        for p in range(4):
            if p != q:
                row = jnp.where(lane == p, pltpu.roll(parts[p], ((p - q) * 32) % 128, 1), row)
        rows.append(row)
    return jnp.concatenate(rows, 0)


def kernel(
    f_hbm, cot_hbm, p_hbm, s_hbm, w_hbm, skip_hbm, tt_hbm, shuffle_hbm, pick_hbm,
    out_hbm, gf_hbm, gw_hbm, gk_hbm,
    f_in, cot_in, p_ref, s_ref, skip_ref, tt_ref, shuffle_ref, pick_ref,
    out_ref, gf_ref, gw_ref, gk_ref,
    fall, gall, wall, act, pbig, sbig, pbig_t, sbig_t, kron1, kron2,
    xs, xr, ys, yr, ms, mr, vs, vr,
    bxs, bxr, bys, byr, bms, bmr, bvs, bvr,
    gws, gwr, k1s, k1r, k2s, k2r, k3r,
    send, recv, local, cot_ref, wall_t, far_sem,
):
    lat = lax.axis_index("lat")
    x = lax.axis_index("ch")
    y, z, core = lat // (Z * K), (lat // K) % Z, lat % K
    b = y * K + core
    me = x * B + b

    def plane_device(s):
        bb = s % B
        return ((bb // K) * (Z * K) + z * K + bb % K, s // B)

    def z_device(zz):
        return (y * (Z * K) + zz * K + core, x)

    def remote(src, dst, slot, device):
        return pltpu.make_async_remote_copy(
            src_ref=src, dst_ref=dst, send_sem=send.at[slot], recv_sem=recv.at[slot],
            device_id=device, device_id_type=MESH,
        )

    def peer(i):
        def ring(k):
            return jnp.where(k == 3, 0, jnp.where(k == 2, 3, 2 - k))

        dx, dy, dc = ring(i // B), ring((i // K) % Y), 1 - i % K
        return ((x + dx) % X) * B + ((y + dy) % Y) * K + (core + dc) % K

    def to_plane(slot, src, dst):
        @pl.loop(0, PLANE - 1, unroll=True)
        def _(i):
            s = peer(i)
            remote(src.at[s], dst.at[me], slot, plane_device(s)).start()

        dst[me] = src[me]

    def far(i):
        half = i // 2
        return jnp.where(i % 2 == 0, Z // 2 + half, Z // 2 - half)

    def to_column(slot, src, dst, indexed):
        @pl.loop(1, Z, unroll=True)
        def _(i):
            zz = lax.rem(z + far(i), Z)
            remote(src.at[zz] if indexed else src, dst.at[z], slot, z_device(zz)).start()

        dst[z] = src[z] if indexed else src[...]

    def wait_recv(slot, dst, count):
        part = dst.at[pl.ds(0, count)]
        pltpu.make_async_copy(part, part, recv.at[slot]).wait()

    def wait_send(slot, dst, count):
        part = dst.at[pl.ds(0, count)]
        pltpu.make_async_copy(part, part, send.at[slot]).wait()

    barrier = pltpu.get_barrier_semaphore()

    near = Z // 4
    for i in range(near, 0, -1):
        for step in (i, Z - i):
            pl.semaphore_signal(
                barrier, inc=1, device_id=z_device(lax.rem(z + step, Z)), device_id_type=MESH
            )

    @pl.loop(0, PLANE - 1, unroll=True)
    def _(i):
        pl.semaphore_signal(
            barrier, inc=1, device_id=plane_device(peer(i)), device_id_type=MESH
        )

    def load(src, dst, slot):
        copy = pltpu.make_async_copy(src, dst, local.at[slot])
        copy.start()
        return copy

    first = ((f_hbm, f_in), (tt_hbm, tt_ref), (shuffle_hbm, shuffle_ref))
    rest = (
        (p_hbm, p_ref), (s_hbm, s_ref), (pick_hbm, pick_ref), (w_hbm.at[0], wall.at[b]),
        (skip_hbm, skip_ref), (cot_hbm, cot_in),
    )
    loads = [load(source, target, i) for i, (source, target) in enumerate(first)]

    def spread(values, dst):
        rounded = values.astype(BF16)
        cat = jnp.concatenate([rounded[32 * jj : 32 * jj + 32] for jj in range(4)], 1)
        for a in range(ROWS):
            dst[:, a, :] = dot(cat, shuffle_ref[:, 128 * a : 128 * a + 128])

    def collect(src):
        cat = jnp.concatenate([src[:, a, :] for a in range(ROWS)], 1).astype(BF16)
        wide = dot_t(cat, shuffle_ref[...])
        tall = jnp.concatenate([wide[:, 128 * jj : 128 * jj + 128] for jj in range(4)], 0)
        return tall.T

    def partial_sums(big, src, dst):
        rows = jnp.concatenate([src[:, a, :] for a in range(ROWS)], 0).astype(BF16)
        dst[...] = dot(big[...], rows).astype(BF16).reshape(Z, 32, 128)

    def total(src):
        acc = src[0].astype(F32)
        for zz in range(1, Z):
            acc = acc + src[zz].astype(F32)
        return swap_blocks(acc)

    def expand_rows(big, src, dst):
        v = dot(big[...], src[...].reshape(512, 128))
        for a in range(ROWS):
            dst[:, a, :] = swap_blocks(v[32 * a : 32 * a + 32])

    def mode_rows(values, mode):
        return jnp.where(iota((32, 128), 0) % 8 == mode, values, 0.0).astype(BF16)

    loads[0].wait()
    fall[x] = f_in[...].reshape(GROUP * ROWS, NLON)
    own = fall.at[x]
    loads[1].wait()
    loads += [load(source, target, 3 + i) for i, (source, target) in enumerate(rest)]
    x_modes = dot_t(tt_ref[...], own[...])
    loads[2].wait()
    spread(x_modes, xs)
    loads[6].wait()
    pl.semaphore_wait(barrier, PLANE - 1 + 2 * near)
    for step in (near, Z - near):
        pl.semaphore_signal(
            far_sem, inc=1, device_id=z_device(lax.rem(z + step, Z)), device_id_type=MESH
        )

    to_plane(0, xs, xr)

    @pl.loop(1, B)
    def _(i):
        bb = lax.rem(b + i, B)
        remote(wall.at[b], wall.at[b], 1, plane_device(x * B + bb)).start()

    parts = ((0, 32), (32, 48), (80, 48))

    def gather_x(slot, ref, k):
        block = ref.at[x, pl.ds(*parts[k])]

        @pl.loop(1, X)
        def _(i):
            remote(block, block, slot + k, (lat, lax.rem(x + i, X))).start()

    def wait_gather(slot, ref):
        for k in range(3):
            part = ref.at[pl.ds(0, X - 1), pl.ds(*parts[k])]
            pltpu.make_async_copy(part, part, recv.at[slot + k]).wait()

    def wait_gather_sent(slot, ref):
        for k in range(3):
            part = ref.at[pl.ds(0, X - 1), pl.ds(*parts[k])]
            pltpu.make_async_copy(part, part, send.at[slot + k]).wait()

    gather_x(15, fall, 0)

    row = iota((128, 512), 0)
    bb = row % B
    pick_a = onehot(
        iota((128, 512), 1) == (bb // K) * (Z * K * ROWS) + (z * K + bb % K) * ROWS + row // 32
    )
    for i in (3, 4, 5):
        loads[i].wait()
    p_rows = dot_t(pick_a, p_ref[...].astype(BF16)).astype(BF16)
    s_rows = dot(pick_a, s_ref[...].astype(BF16)).astype(BF16)
    same = (iota((512, 128), 0) // 8) % 4 == (iota((512, 128), 1) // 8) % 4
    same_t = (iota((128, 512), 0) // 8) % 4 == (iota((128, 512), 1) // 8) % 4
    pick = pick_ref[...]
    pbig[...] = jnp.where(same, dot_t(pick, p_rows), 0.0).astype(BF16)
    sbig[...] = jnp.where(same_t, dot_t(s_rows, pick), 0.0).astype(BF16)
    sbig_t[...] = jnp.where(same, dot_t(pick, s_rows), 0.0).astype(BF16)
    pbig_t[...] = jnp.where(same_t, dot_t(p_rows, pick), 0.0).astype(BF16)

    wait_recv(0, xr, PLANE - 1)
    partial_sums(pbig, xr, ys)
    pl.semaphore_wait(far_sem, 2)
    to_column(3, ys, yr, True)
    gather_x(15, fall, 1)

    loads[7].wait()
    pick_g = onehot(iota((128, 128), 1) == x * GROUP + iota((128, 128), 0) // ROWS)
    each = onehot(iota((128, 512), 0) == iota((128, 512), 1) // ROWS)
    same_row = iota((128, 512), 0) % ROWS == iota((128, 512), 1) % ROWS
    skip = skip_ref[...]
    kron1[...] = jnp.where(same_row, dot(dot_t(pick_g, skip).astype(BF16), each), 0.0).astype(BF16)
    kron2[...] = jnp.where(same_row, dot(dot(pick_g, skip).astype(BF16), each), 0.0).astype(BF16)

    loads[8].wait()
    cot_ref[...] = cot_in[...].reshape(GROUP * ROWS, NLON)

    wait_recv(1, wall, B - 1)
    wait_recv(3, yr, Z - 1)
    spectral = total(yr).astype(BF16).astype(F32)
    w0 = wall[:, 0].reshape(B * C, C)
    w1 = wall[:, 1].reshape(B * C, C)
    wide = jnp.concatenate([mode_rows(spectral, m) for m in range(B)], 1)
    r0, r1 = dot(wide, w0), dot(wide, w1)
    mixed = jnp.concatenate([r0[:16] - r1[16:], r0[16:] + r1[:16]], 0)
    ms[...] = mixed.astype(BF16)
    to_column(4, ms, mr, False)
    gather_x(15, fall, 2)
    for jj in range(4):
        gws[:, jj, :] = spectral[8 * jj : 8 * jj + 8]

    for m in range(B):
        for part in range(2):
            wall_t[part, 128 * m : 128 * m + 128] = wall[m, part].T

    wait_recv(4, mr, Z - 1)
    expand_rows(sbig, mr, vs)
    to_plane(5, vs, vr)

    wait_gather(15, fall)
    acc = dot(kron1[:, 0:128], fall[0])
    for g in range(1, X):
        acc = acc + dot(kron1[:, 128 * g : 128 * g + 128], fall[g])
    act[...] = acc

    col = iota((128, 128), 1) % M
    doubling = jnp.where(col == 0, 1.0, 2.0)
    wait_recv(5, vr, PLANE - 1)
    v_modes = (collect(vr) * doubling).astype(BF16)
    act[...] += dot(v_modes, tt_ref[...])

    scale = math.sqrt(2.0 / math.pi)

    g_ref = gall.at[x]

    @pl.loop(0, 128 // CHUNK)
    def _(i):
        rows = pl.ds(pl.multiple_of(i * CHUNK, CHUNK), CHUNK)
        u = act[rows, :]
        square = u * u
        t = jnp.tanh(scale * u * (1.0 + 0.044715 * square))
        cdf = 0.5 * (1.0 + t)
        out_ref[rows, :] = (u * cdf).astype(BF16)
        slope = cdf + 0.5 * u * (1.0 - t * t) * (scale * (1.0 + 3 * 0.044715 * square))
        g_ref[rows, :] = (cot_ref[rows, :].astype(F32) * slope).astype(BF16)

    g_pre = g_ref[...]
    row = iota((128, 128), 0) % M
    doubling_t = jnp.where(row == 0, 1.0, 2.0)
    spread(dot_t(tt_ref[...], g_pre) * doubling_t, bxs)
    to_plane(6, bxs, bxr)
    gather_x(18, gall, 0)

    f_in[...] = out_ref[...].reshape(GROUP, ROWS, NLON)
    store_out = load(f_in, out_hbm, 0)

    same_lane = iota((128, 128), 0) % ROWS == iota((128, 128), 1) % ROWS
    term = jnp.zeros((128, 128), F32)
    for g in range(X):
        full = jnp.where(same_lane, dot_t(g_pre, fall[g]), 0.0)
        lanes = jnp.where(iota((128, 128), 1) == GROUP * g + iota((128, 128), 0) // ROWS, 1.0, 0.0)
        term = term + jnp.dot(
            full, lanes, precision=lax.Precision.HIGHEST, preferred_element_type=F32
        )
    fold = jnp.where(iota((32, 128), 0) == iota((32, 128), 1) // ROWS, 1.0, 0.0)
    term = jnp.dot(fold, term, precision=lax.Precision.HIGHEST, preferred_element_type=F32)
    for i in range(ROWS):
        k1s[:, i, :] = term[8 * i : 8 * i + 8]

    @pl.loop(1, B)
    def _(i):
        bb = lax.rem(b + i, B)
        remote(k1s.at[bb], k1r.at[b], 9, plane_device(x * B + bb)).start()

    k1r[b] = k1s[b]

    wait_recv(6, bxr, PLANE - 1)
    partial_sums(sbig_t, bxr, bys)
    to_column(8, bys, byr, True)
    gather_x(18, gall, 1)

    wait_recv(9, k1r, B - 1)
    acc = k1r[0]
    for i in range(1, B):
        acc = acc + k1r[i]
    k2s[...] = acc

    wait_recv(8, byr, Z - 1)
    g_mixed = total(byr).astype(BF16).astype(F32)
    wide = jnp.concatenate([mode_rows(g_mixed, m) for m in range(B)], 1)
    r0, r1 = dot(wide, wall_t[0]), dot(wide, wall_t[1])
    g_spectral = jnp.concatenate([r0[:16] + r1[16:], r0[16:] - r1[:16]], 0)
    bms[...] = g_spectral.astype(BF16)
    to_column(10, bms, bmr, False)

    @pl.loop(1, Z, unroll=True)
    def _(i):
        zz = lax.rem(z + far(i), Z)
        remote(k2s, k2r.at[z], 12, z_device(zz)).start()

    k2r[z] = k2s[...]

    for jj in range(4):
        gws[:, 4 + jj, :] = g_mixed[8 * jj : 8 * jj + 8]

    @pl.loop(1, PLANE)
    def _(i):
        s = lax.rem(me + i, PLANE)
        remote(gws.at[s % B], gwr.at[me], 11, plane_device(s)).start()

    gwr[me] = gws[b]
    gather_x(18, gall, 2)

    wait_recv(11, gwr, PLANE - 1)
    s_all = jnp.concatenate([gwr[:, jj, :] for jj in range(4)], 0).astype(BF16)
    g_all = jnp.concatenate([gwr[:, 4 + jj, :] for jj in range(4)], 0).astype(BF16)
    pick_o = onehot(iota((GROUP, 128), 1) == x * GROUP + iota((GROUP, 128), 0))
    g_own = dot_t(pick_o, g_all)
    g_turn = jnp.concatenate([g_own[:, 64:], -g_own[:, :64]], 1)
    gw_ref[0] = dot(g_own.astype(BF16), s_all) * (1.0 / math.sqrt(2 * M))
    gw_ref[1] = dot(g_turn.astype(BF16), s_all) * (1.0 / math.sqrt(2 * M))
    store_gw = load(gw_ref, gw_hbm, 1)

    wait_recv(10, bmr, Z - 1)
    expand_rows(pbig_t, bmr, bvs)
    to_plane(13, bvs, bvr)

    wait_recv(12, k2r, Z - 1)
    acc = k2r[0]
    for i in range(1, Z):
        acc = acc + k2r[i]
    k3r[b] = acc * (1.0 / math.sqrt(Y * Z * K * ROWS * NLON))

    @pl.loop(1, B)
    def _(i):
        bb = lax.rem(b + i, B)
        remote(k3r.at[b], k3r.at[b], 14, plane_device(x * B + bb)).start()

    wait_gather(18, gall)
    acc = dot(kron2[:, 0:128], gall[0])
    for g in range(1, X):
        acc = acc + dot(kron2[:, 128 * g : 128 * g + 128], gall[g])
    act[...] = acc

    wait_recv(14, k3r, B - 1)
    gk_ref[...] = jnp.concatenate([k3r[:, i, :] for i in range(ROWS)], 0)
    store_gk = load(gk_ref, gk_hbm, 2)

    wait_recv(13, bvr, PLANE - 1)
    modes = collect(bvr).astype(BF16)
    stores = [store_out, store_gw, store_gk]
    for i in range(4):
        part = act[32 * i : 32 * i + 32] + dot(modes[32 * i : 32 * i + 32], tt_ref[...])
        held = gf_ref.at[pl.ds(8 * i, 8)]
        held[...] = part.reshape(8, ROWS, NLON).astype(BF16)
        stores.append(load(held, gf_hbm.at[pl.ds(8 * i, 8)], 3 + i))

    wait_send(0, xs, PLANE - 1)
    wait_send(1, wall, B - 1)
    wait_gather_sent(15, fall)
    wait_send(3, ys, Z - 1)
    wait_send(4, mr, Z - 1)
    wait_send(5, vs, PLANE - 1)
    wait_send(6, bxs, PLANE - 1)
    wait_gather_sent(18, gall)
    wait_send(8, bys, Z - 1)
    wait_send(9, k1s, B - 1)
    wait_send(10, bmr, Z - 1)
    wait_send(11, gwr, PLANE - 1)
    wait_send(12, k2r, Z - 1)
    wait_send(13, bvs, PLANE - 1)
    wait_send(14, k3r, B - 1)
    for copy in stores:
        copy.wait()


def copy_out(*refs):
    sources, targets, held = refs[:4], refs[4:8], refs[8:12]
    loaded, stored = refs[12:]
    loads = [pltpu.make_async_copy(sources[i], held[i], loaded.at[i]) for i in range(4)]
    stores = [pltpu.make_async_copy(held[i], targets[i], stored.at[i]) for i in range(4)]
    for load in loads:
        load.start()
    for load, store in zip(loads, stores):
        load.wait()
        store.start()
    for store in stores:
        store.wait()


def on_device(features, projection, synthesis, mode_weights, skip_weights, cotangent):
    anywhere = pl.BlockSpec(memory_space=pl.ANY)
    plane = pltpu.VMEM((PLANE, ROWS, 128), F32)
    column = pltpu.VMEM((Z, 32, 128), BF16)
    one = pltpu.VMEM((32, 128), BF16)
    tall = pltpu.VMEM((512, 128), BF16)
    flat = pltpu.VMEM((128, 512), BF16)
    field = pltpu.VMEM((X, GROUP * ROWS, NLON), BF16)
    phases = [plane, plane, column, column, one, column, plane, plane]
    results = (
        jax.ShapeDtypeStruct((GROUP, ROWS, NLON), BF16),
        jax.ShapeDtypeStruct((GROUP, ROWS, NLON), BF16),
        jax.ShapeDtypeStruct((2, GROUP, C), F32),
        jax.ShapeDtypeStruct((GROUP, C), F32),
    )
    kept = pl.pallas_call(
        kernel,
        out_shape=results,
        in_specs=[anywhere] * 9,
        out_specs=[anywhere] * 4,
        scratch_shapes=[
            pltpu.VMEM((GROUP, ROWS, NLON), BF16),
            pltpu.VMEM((GROUP, ROWS, NLON), BF16),
            pltpu.VMEM((C, 512), F32),
            pltpu.VMEM((512, C), F32),
            pltpu.VMEM((C, C), BF16),
            pltpu.VMEM((C, NLON), BF16),
            pltpu.VMEM((512, 512), BF16),
            pltpu.VMEM((512, C), BF16),
            pltpu.VMEM((GROUP * ROWS, NLON), BF16),
            pltpu.VMEM((GROUP, ROWS, NLON), BF16),
            pltpu.VMEM((2, GROUP, C), F32),
            pltpu.VMEM((GROUP, C), F32),
            field,
            field,
            pltpu.VMEM((B, 2, C, C), BF16),
            pltpu.VMEM((GROUP * ROWS, NLON), F32),
            tall, flat, flat, tall, flat, flat,
            *phases,
            *phases,
            pltpu.VMEM((B, 8, 128), F32),
            pltpu.VMEM((PLANE, 8, 128), F32),
            pltpu.VMEM((B, ROWS, 128), F32),
            pltpu.VMEM((B, ROWS, 128), F32),
            pltpu.VMEM((ROWS, 128), F32),
            pltpu.VMEM((Z, ROWS, 128), F32),
            pltpu.VMEM((B, ROWS, 128), F32),
            pltpu.SemaphoreType.DMA((21,)),
            pltpu.SemaphoreType.DMA((21,)),
            pltpu.SemaphoreType.DMA((9,)),
            pltpu.VMEM((GROUP * ROWS, NLON), BF16),
            pltpu.VMEM((2, B * C, C), BF16),
            pltpu.SemaphoreType.REGULAR,
        ],
        compiler_params=pltpu.CompilerParams(
            collective_id=0, has_side_effects=True, vmem_limit_bytes=56 * 1024 * 1024
        ),
    )(
        features,
        cotangent,
        projection,
        synthesis,
        mode_weights,
        skip_weights,
        fourier_table(),
        shuffle_table(),
        row_table(),
    )
    out, grad_features, grad_weights, grad_skip = pl.pallas_call(
        copy_out,
        out_shape=results,
        in_specs=[anywhere] * 4,
        out_specs=[anywhere] * 4,
        scratch_shapes=[
            *[pltpu.VMEM(r.shape, r.dtype) for r in results],
            pltpu.SemaphoreType.DMA((4,)),
            pltpu.SemaphoreType.DMA((4,)),
        ],
        compiler_params=pltpu.CompilerParams(vmem_limit_bytes=56 * 1024 * 1024),
        name="copy_out",
    )(*kept)
    return (out, grad_features, grad_weights.transpose(0, 2, 1)[None], grad_skip.T)


def solution(mesh):
    placed = (P("ch", "lat", None), P(), P(), P("lat", None, None, None), P(), P("ch", "lat", None))
    return jax.shard_map(
        on_device,
        mesh=mesh,
        in_specs=placed,
        out_specs=(
            P("ch", "lat", None),
            P("ch", "lat", None),
            P("lat", None, None, "ch"),
            P(None, "ch"),
        ),
        check_vma=False,
    )
```

```python
import math

import jax
import jax.numpy as jnp
import numpy as np
from jax import lax
from jax.experimental import pallas as pl
from jax.experimental.pallas import tpu as pltpu
from jax.sharding import PartitionSpec as P

MESH = pl.DeviceIdType.MESH
F32 = jnp.float32
BF16 = jnp.bfloat16

M = 64
NLON = 1440
C = 128
X, Y, Z, K = 4, 4, 16, 2
B = Y * K
PLANE = X * B
GROUP = C // X
ROWS = 4
CHUNK = 16


def fourier_table():
    column = np.arange(NLON)
    mode = np.arange(M)
    phase = (mode[:, None] * column[None, :] % NLON) * (2.0 * math.pi / NLON)
    table = np.concatenate([np.cos(phase), -np.sin(phase)], 0) / math.sqrt(NLON)
    return jnp.asarray(table.astype(np.float32), BF16)


def shuffle_table():
    table = np.zeros((ROWS, GROUP, ROWS, ROWS, ROWS, GROUP), np.float32)
    for jj in range(4):
        for c in range(GROUP):
            for a in range(ROWS):
                table[jj, c, a, a, jj, c] = 1
    return jnp.asarray(table.reshape(512, 512), BF16)


def row_table():
    table = np.zeros((Z, X, B, C), np.float32)
    for z in range(Z):
        for b in range(B):
            table[z, :, b, (b // K) * Z * K + z * K + b % K] = 1
    return jnp.asarray(table.reshape(512, C), BF16)


def iota(shape, dim):
    return lax.broadcasted_iota(jnp.int32, shape, dim)


def dot(left, right):
    return jnp.dot(left, right, preferred_element_type=F32)


def dot_t(left, right):
    return lax.dot_general(left, right, (((1,), (1,)), ((), ())), preferred_element_type=F32)


def onehot(mask):
    return jnp.where(mask, 1.0, 0.0).astype(BF16)


def swap_blocks(v):
    lane = iota((8, 128), 1) // 32
    parts = [v[8 * p : 8 * p + 8] for p in range(4)]
    rows = []
    for q in range(4):
        row = parts[q]
        for p in range(4):
            if p != q:
                row = jnp.where(lane == p, pltpu.roll(parts[p], ((p - q) * 32) % 128, 1), row)
        rows.append(row)
    return jnp.concatenate(rows, 0)


def kernel(
    f_hbm, cot_hbm, p_hbm, s_hbm, w_hbm, skip_hbm, tt_hbm, shuffle_hbm, pick_hbm,
    out_hbm, gf_hbm, gw_hbm, gk_hbm,
    f_in, cot_in, p_ref, s_ref, skip_ref, tt_ref, shuffle_ref, pick_ref,
    out_ref, gf_ref, gw_ref, gk_ref,
    fall, gall, wall, act, pbig, sbig, pbig_t, sbig_t, kron1, kron2,
    xs, xr, ys, yr, ms, mr, vs, vr,
    bxs, bxr, bys, byr, bms, bmr, bvs, bvr,
    gws, gwr, k1s, k1r, k2s, k2r, k3r,
    send, recv, local, cot_ref, wall_t, far_sem,
):
    lat = lax.axis_index("lat")
    x = lax.axis_index("ch")
    y, z, core = lat // (Z * K), (lat // K) % Z, lat % K
    b = y * K + core
    me = x * B + b

    def plane_device(s):
        bb = s % B
        return ((bb // K) * (Z * K) + z * K + bb % K, s // B)

    def z_device(zz):
        return (y * (Z * K) + zz * K + core, x)

    def remote(src, dst, slot, device):
        return pltpu.make_async_remote_copy(
            src_ref=src, dst_ref=dst, send_sem=send.at[slot], recv_sem=recv.at[slot],
            device_id=device, device_id_type=MESH,
        )

    def peer(i):
        def ring(k):
            return jnp.where(k == 3, 0, jnp.where(k == 2, 3, 2 - k))

        dx, dy, dc = ring(i // B), ring((i // K) % Y), 1 - i % K
        return ((x + dx) % X) * B + ((y + dy) % Y) * K + (core + dc) % K

    def to_plane(slot, src, dst):
        @pl.loop(0, PLANE - 1, unroll=True)
        def _(i):
            s = peer(i)
            remote(src.at[s], dst.at[me], slot, plane_device(s)).start()

        dst[me] = src[me]

    def far(i):
        half = i // 2
        return jnp.where(i % 2 == 0, Z // 2 + half, Z // 2 - half)

    def to_column(slot, src, dst, indexed):
        @pl.loop(1, Z, unroll=True)
        def _(i):
            zz = lax.rem(z + far(i), Z)
            remote(src.at[zz] if indexed else src, dst.at[z], slot, z_device(zz)).start()

        dst[z] = src[z] if indexed else src[...]

    def wait_recv(slot, dst, count):
        part = dst.at[pl.ds(0, count)]
        pltpu.make_async_copy(part, part, recv.at[slot]).wait()

    def wait_send(slot, dst, count):
        part = dst.at[pl.ds(0, count)]
        pltpu.make_async_copy(part, part, send.at[slot]).wait()

    barrier = pltpu.get_barrier_semaphore()

    near = Z // 4
    for i in range(near, 0, -1):
        for step in (i, Z - i):
            pl.semaphore_signal(
                barrier, inc=1, device_id=z_device(lax.rem(z + step, Z)), device_id_type=MESH
            )

    @pl.loop(0, PLANE - 1, unroll=True)
    def _(i):
        pl.semaphore_signal(
            barrier, inc=1, device_id=plane_device(peer(i)), device_id_type=MESH
        )

    def load(src, dst, slot):
        copy = pltpu.make_async_copy(src, dst, local.at[slot])
        copy.start()
        return copy

    first = ((f_hbm, f_in), (tt_hbm, tt_ref), (shuffle_hbm, shuffle_ref))
    rest = (
        (p_hbm, p_ref), (s_hbm, s_ref), (pick_hbm, pick_ref), (w_hbm.at[0], wall.at[b]),
        (skip_hbm, skip_ref), (cot_hbm, cot_in),
    )
    loads = [load(source, target, i) for i, (source, target) in enumerate(first)]

    def spread(values, dst):
        rounded = values.astype(BF16)
        cat = jnp.concatenate([rounded[32 * jj : 32 * jj + 32] for jj in range(4)], 1)
        for a in range(ROWS):
            dst[:, a, :] = dot(cat, shuffle_ref[:, 128 * a : 128 * a + 128])

    def collect(src):
        cat = jnp.concatenate([src[:, a, :] for a in range(ROWS)], 1).astype(BF16)
        wide = dot_t(cat, shuffle_ref[...])
        tall = jnp.concatenate([wide[:, 128 * jj : 128 * jj + 128] for jj in range(4)], 0)
        return tall.T

    def partial_sums(big, src, dst):
        rows = jnp.concatenate([src[:, a, :] for a in range(ROWS)], 0).astype(BF16)
        dst[...] = dot(big[...], rows).astype(BF16).reshape(Z, 32, 128)

    def total(src):
        acc = src[0].astype(F32)
        for zz in range(1, Z):
            acc = acc + src[zz].astype(F32)
        return swap_blocks(acc)

    def expand_rows(big, src, dst):
        v = dot(big[...], src[...].reshape(512, 128))
        for a in range(ROWS):
            dst[:, a, :] = swap_blocks(v[32 * a : 32 * a + 32])

    def mode_rows(values, mode):
        return jnp.where(iota((32, 128), 0) % 8 == mode, values, 0.0).astype(BF16)

    loads[0].wait()
    fall[x] = f_in[...].reshape(GROUP * ROWS, NLON)
    own = fall.at[x]
    loads[1].wait()
    loads += [load(source, target, 3 + i) for i, (source, target) in enumerate(rest)]
    x_modes = dot_t(tt_ref[...], own[...])
    loads[2].wait()
    spread(x_modes, xs)
    loads[6].wait()
    pl.semaphore_wait(barrier, PLANE - 1 + 2 * near)
    for step in (near, Z - near):
        pl.semaphore_signal(
            far_sem, inc=1, device_id=z_device(lax.rem(z + step, Z)), device_id_type=MESH
        )

    to_plane(0, xs, xr)

    @pl.loop(1, B)
    def _(i):
        bb = lax.rem(b + i, B)
        remote(wall.at[b], wall.at[b], 1, plane_device(x * B + bb)).start()

    parts = ((0, 32), (32, 48), (80, 48))

    def gather_x(slot, ref, k):
        block = ref.at[x, pl.ds(*parts[k])]

        @pl.loop(1, X)
        def _(i):
            remote(block, block, slot + k, (lat, lax.rem(x + i, X))).start()

    def wait_gather(slot, ref):
        for k in range(3):
            part = ref.at[pl.ds(0, X - 1), pl.ds(*parts[k])]
            pltpu.make_async_copy(part, part, recv.at[slot + k]).wait()

    def wait_gather_sent(slot, ref):
        for k in range(3):
            part = ref.at[pl.ds(0, X - 1), pl.ds(*parts[k])]
            pltpu.make_async_copy(part, part, send.at[slot + k]).wait()

    gather_x(15, fall, 0)

    row = iota((128, 512), 0)
    bb = row % B
    pick_a = onehot(
        iota((128, 512), 1) == (bb // K) * (Z * K * ROWS) + (z * K + bb % K) * ROWS + row // 32
    )
    for i in (3, 4, 5):
        loads[i].wait()
    p_rows = dot_t(pick_a, p_ref[...].astype(BF16)).astype(BF16)
    s_rows = dot(pick_a, s_ref[...].astype(BF16)).astype(BF16)
    same = (iota((512, 128), 0) // 8) % 4 == (iota((512, 128), 1) // 8) % 4
    same_t = (iota((128, 512), 0) // 8) % 4 == (iota((128, 512), 1) // 8) % 4
    pick = pick_ref[...]
    pbig[...] = jnp.where(same, dot_t(pick, p_rows), 0.0).astype(BF16)
    sbig[...] = jnp.where(same_t, dot_t(s_rows, pick), 0.0).astype(BF16)
    sbig_t[...] = jnp.where(same, dot_t(pick, s_rows), 0.0).astype(BF16)
    pbig_t[...] = jnp.where(same_t, dot_t(p_rows, pick), 0.0).astype(BF16)

    wait_recv(0, xr, PLANE - 1)
    partial_sums(pbig, xr, ys)
    pl.semaphore_wait(far_sem, 2)
    to_column(3, ys, yr, True)
    gather_x(15, fall, 1)

    loads[7].wait()
    pick_g = onehot(iota((128, 128), 1) == x * GROUP + iota((128, 128), 0) // ROWS)
    each = onehot(iota((128, 512), 0) == iota((128, 512), 1) // ROWS)
    same_row = iota((128, 512), 0) % ROWS == iota((128, 512), 1) % ROWS
    skip = skip_ref[...]
    kron1[...] = jnp.where(same_row, dot(dot_t(pick_g, skip).astype(BF16), each), 0.0).astype(BF16)
    kron2[...] = jnp.where(same_row, dot(dot(pick_g, skip).astype(BF16), each), 0.0).astype(BF16)

    loads[8].wait()
    cot_ref[...] = cot_in[...].reshape(GROUP * ROWS, NLON)

    wait_recv(1, wall, B - 1)
    wait_recv(3, yr, Z - 1)
    spectral = total(yr).astype(BF16).astype(F32)
    w0 = wall[:, 0].reshape(B * C, C)
    w1 = wall[:, 1].reshape(B * C, C)
    wide = jnp.concatenate([mode_rows(spectral, m) for m in range(B)], 1)
    r0, r1 = dot(wide, w0), dot(wide, w1)
    mixed = jnp.concatenate([r0[:16] - r1[16:], r0[16:] + r1[:16]], 0)
    ms[...] = mixed.astype(BF16)
    to_column(4, ms, mr, False)
    gather_x(15, fall, 2)
    for jj in range(4):
        gws[:, jj, :] = spectral[8 * jj : 8 * jj + 8]

    for m in range(B):
        for part in range(2):
            wall_t[part, 128 * m : 128 * m + 128] = wall[m, part].T

    wait_recv(4, mr, Z - 1)
    expand_rows(sbig, mr, vs)
    to_plane(5, vs, vr)

    wait_gather(15, fall)
    acc = dot(kron1[:, 0:128], fall[0])
    for g in range(1, X):
        acc = acc + dot(kron1[:, 128 * g : 128 * g + 128], fall[g])
    act[...] = acc

    col = iota((128, 128), 1) % M
    doubling = jnp.where(col == 0, 1.0, 2.0)
    wait_recv(5, vr, PLANE - 1)
    v_modes = (collect(vr) * doubling).astype(BF16)
    act[...] += dot(v_modes, tt_ref[...])

    scale = math.sqrt(2.0 / math.pi)

    g_ref = gall.at[x]

    @pl.loop(0, 128 // CHUNK)
    def _(i):
        rows = pl.ds(pl.multiple_of(i * CHUNK, CHUNK), CHUNK)
        u = act[rows, :]
        square = u * u
        t = jnp.tanh(scale * u * (1.0 + 0.044715 * square))
        cdf = 0.5 * (1.0 + t)
        out_ref[rows, :] = (u * cdf).astype(BF16)
        slope = cdf + 0.5 * u * (1.0 - t * t) * (scale * (1.0 + 3 * 0.044715 * square))
        g_ref[rows, :] = (cot_ref[rows, :].astype(F32) * slope).astype(BF16)

    g_pre = g_ref[...]
    row = iota((128, 128), 0) % M
    doubling_t = jnp.where(row == 0, 1.0, 2.0)
    spread(dot_t(tt_ref[...], g_pre) * doubling_t, bxs)
    to_plane(6, bxs, bxr)
    gather_x(18, gall, 0)

    f_in[...] = out_ref[...].reshape(GROUP, ROWS, NLON)
    store_out = load(f_in, out_hbm, 0)

    same_lane = iota((128, 128), 0) % ROWS == iota((128, 128), 1) % ROWS
    term = jnp.zeros((128, 128), F32)
    for g in range(X):
        full = jnp.where(same_lane, dot_t(g_pre, fall[g]), 0.0)
        lanes = jnp.where(iota((128, 128), 1) == GROUP * g + iota((128, 128), 0) // ROWS, 1.0, 0.0)
        term = term + jnp.dot(
            full, lanes, precision=lax.Precision.HIGHEST, preferred_element_type=F32
        )
    fold = jnp.where(iota((32, 128), 0) == iota((32, 128), 1) // ROWS, 1.0, 0.0)
    term = jnp.dot(fold, term, precision=lax.Precision.HIGHEST, preferred_element_type=F32)
    for i in range(ROWS):
        k1s[:, i, :] = term[8 * i : 8 * i + 8]

    @pl.loop(1, B)
    def _(i):
        bb = lax.rem(b + i, B)
        remote(k1s.at[bb], k1r.at[b], 9, plane_device(x * B + bb)).start()

    k1r[b] = k1s[b]

    wait_recv(6, bxr, PLANE - 1)
    partial_sums(sbig_t, bxr, bys)
    to_column(8, bys, byr, True)
    gather_x(18, gall, 1)

    wait_recv(9, k1r, B - 1)
    acc = k1r[0]
    for i in range(1, B):
        acc = acc + k1r[i]
    k2s[...] = acc

    wait_recv(8, byr, Z - 1)
    g_mixed = total(byr).astype(BF16).astype(F32)
    wide = jnp.concatenate([mode_rows(g_mixed, m) for m in range(B)], 1)
    r0, r1 = dot(wide, wall_t[0]), dot(wide, wall_t[1])
    g_spectral = jnp.concatenate([r0[:16] + r1[16:], r0[16:] - r1[:16]], 0)
    bms[...] = g_spectral.astype(BF16)
    to_column(10, bms, bmr, False)

    @pl.loop(1, Z, unroll=True)
    def _(i):
        zz = lax.rem(z + far(i), Z)
        remote(k2s, k2r.at[z], 12, z_device(zz)).start()

    k2r[z] = k2s[...]

    for jj in range(4):
        gws[:, 4 + jj, :] = g_mixed[8 * jj : 8 * jj + 8]

    @pl.loop(1, PLANE)
    def _(i):
        s = lax.rem(me + i, PLANE)
        remote(gws.at[s % B], gwr.at[me], 11, plane_device(s)).start()

    gwr[me] = gws[b]
    gather_x(18, gall, 2)

    wait_recv(11, gwr, PLANE - 1)
    s_all = jnp.concatenate([gwr[:, jj, :] for jj in range(4)], 0).astype(BF16)
    g_all = jnp.concatenate([gwr[:, 4 + jj, :] for jj in range(4)], 0).astype(BF16)
    pick_o = onehot(iota((GROUP, 128), 1) == x * GROUP + iota((GROUP, 128), 0))
    g_own = dot_t(pick_o, g_all)
    g_turn = jnp.concatenate([g_own[:, 64:], -g_own[:, :64]], 1)
    gw_ref[0] = dot(g_own.astype(BF16), s_all) * (1.0 / math.sqrt(2 * M))
    gw_ref[1] = dot(g_turn.astype(BF16), s_all) * (1.0 / math.sqrt(2 * M))
    store_gw = load(gw_ref, gw_hbm, 1)

    wait_recv(10, bmr, Z - 1)
    expand_rows(pbig_t, bmr, bvs)
    to_plane(13, bvs, bvr)

    wait_recv(12, k2r, Z - 1)
    acc = k2r[0]
    for i in range(1, Z):
        acc = acc + k2r[i]
    k3r[b] = acc * (1.0 / math.sqrt(Y * Z * K * ROWS * NLON))

    @pl.loop(1, B)
    def _(i):
        bb = lax.rem(b + i, B)
        remote(k3r.at[b], k3r.at[b], 14, plane_device(x * B + bb)).start()

    wait_gather(18, gall)
    acc = dot(kron2[:, 0:128], gall[0])
    for g in range(1, X):
        acc = acc + dot(kron2[:, 128 * g : 128 * g + 128], gall[g])
    act[...] = acc

    wait_recv(14, k3r, B - 1)
    gk_ref[...] = jnp.concatenate([k3r[:, i, :] for i in range(ROWS)], 0)
    store_gk = load(gk_ref, gk_hbm, 2)

    wait_recv(13, bvr, PLANE - 1)
    modes = collect(bvr).astype(BF16)
    stores = [store_out, store_gw, store_gk]
    for i in range(4):
        part = act[32 * i : 32 * i + 32] + dot(modes[32 * i : 32 * i + 32], tt_ref[...])
        held = gf_ref.at[pl.ds(8 * i, 8)]
        held[...] = part.reshape(8, ROWS, NLON).astype(BF16)
        stores.append(load(held, gf_hbm.at[pl.ds(8 * i, 8)], 3 + i))

    wait_send(0, xs, PLANE - 1)
    wait_send(1, wall, B - 1)
    wait_gather_sent(15, fall)
    wait_send(3, ys, Z - 1)
    wait_send(4, mr, Z - 1)
    wait_send(5, vs, PLANE - 1)
    wait_send(6, bxs, PLANE - 1)
    wait_gather_sent(18, gall)
    wait_send(8, bys, Z - 1)
    wait_send(9, k1s, B - 1)
    wait_send(10, bmr, Z - 1)
    wait_send(11, gwr, PLANE - 1)
    wait_send(12, k2r, Z - 1)
    wait_send(13, bvs, PLANE - 1)
    wait_send(14, k3r, B - 1)
    for copy in stores:
        copy.wait()


def copy_out(*refs):
    sources, targets, held = refs[:4], refs[4:8], refs[8:12]
    loaded, stored = refs[12:]
    loads, stores = [], []
    for i in range(4):
        step = GROUP // 4
        for part in [pl.ds(k * step, step) for k in range(4)] if i < 2 else [pl.ds(0, held[i].shape[0])]:
            n = len(loads)
            here = held[i].at[part]
            loads.append(pltpu.make_async_copy(sources[i].at[part], here, loaded.at[n]))
            stores.append(pltpu.make_async_copy(here, targets[i].at[part], stored.at[n]))
    for load in loads:
        load.start()
    for load, store in zip(loads, stores):
        load.wait()
        store.start()
    for store in stores:
        store.wait()


def on_device(features, projection, synthesis, mode_weights, skip_weights, cotangent):
    anywhere = pl.BlockSpec(memory_space=pl.ANY)
    plane = pltpu.VMEM((PLANE, ROWS, 128), F32)
    column = pltpu.VMEM((Z, 32, 128), BF16)
    one = pltpu.VMEM((32, 128), BF16)
    tall = pltpu.VMEM((512, 128), BF16)
    flat = pltpu.VMEM((128, 512), BF16)
    field = pltpu.VMEM((X, GROUP * ROWS, NLON), BF16)
    phases = [plane, plane, column, column, one, column, plane, plane]
    results = (
        jax.ShapeDtypeStruct((GROUP, ROWS, NLON), BF16),
        jax.ShapeDtypeStruct((GROUP, ROWS, NLON), BF16),
        jax.ShapeDtypeStruct((2, GROUP, C), F32),
        jax.ShapeDtypeStruct((GROUP, C), F32),
    )
    kept = pl.pallas_call(
        kernel,
        out_shape=results,
        in_specs=[anywhere] * 9,
        out_specs=[anywhere] * 4,
        scratch_shapes=[
            pltpu.VMEM((GROUP, ROWS, NLON), BF16),
            pltpu.VMEM((GROUP, ROWS, NLON), BF16),
            pltpu.VMEM((C, 512), F32),
            pltpu.VMEM((512, C), F32),
            pltpu.VMEM((C, C), BF16),
            pltpu.VMEM((C, NLON), BF16),
            pltpu.VMEM((512, 512), BF16),
            pltpu.VMEM((512, C), BF16),
            pltpu.VMEM((GROUP * ROWS, NLON), BF16),
            pltpu.VMEM((GROUP, ROWS, NLON), BF16),
            pltpu.VMEM((2, GROUP, C), F32),
            pltpu.VMEM((GROUP, C), F32),
            field,
            field,
            pltpu.VMEM((B, 2, C, C), BF16),
            pltpu.VMEM((GROUP * ROWS, NLON), F32),
            tall, flat, flat, tall, flat, flat,
            *phases,
            *phases,
            pltpu.VMEM((B, 8, 128), F32),
            pltpu.VMEM((PLANE, 8, 128), F32),
            pltpu.VMEM((B, ROWS, 128), F32),
            pltpu.VMEM((B, ROWS, 128), F32),
            pltpu.VMEM((ROWS, 128), F32),
            pltpu.VMEM((Z, ROWS, 128), F32),
            pltpu.VMEM((B, ROWS, 128), F32),
            pltpu.SemaphoreType.DMA((21,)),
            pltpu.SemaphoreType.DMA((21,)),
            pltpu.SemaphoreType.DMA((9,)),
            pltpu.VMEM((GROUP * ROWS, NLON), BF16),
            pltpu.VMEM((2, B * C, C), BF16),
            pltpu.SemaphoreType.REGULAR,
        ],
        compiler_params=pltpu.CompilerParams(
            collective_id=0, has_side_effects=True, vmem_limit_bytes=56 * 1024 * 1024
        ),
    )(
        features,
        cotangent,
        projection,
        synthesis,
        mode_weights,
        skip_weights,
        fourier_table(),
        shuffle_table(),
        row_table(),
    )
    out, grad_features, grad_weights, grad_skip = pl.pallas_call(
        copy_out,
        out_shape=results,
        in_specs=[anywhere] * 4,
        out_specs=[anywhere] * 4,
        scratch_shapes=[
            *[pltpu.VMEM(r.shape, r.dtype) for r in results],
            pltpu.SemaphoreType.DMA((10,)),
            pltpu.SemaphoreType.DMA((10,)),
        ],
        compiler_params=pltpu.CompilerParams(vmem_limit_bytes=56 * 1024 * 1024),
        name="copy_out",
    )(*kept)
    return (out, grad_features, grad_weights.transpose(0, 2, 1)[None], grad_skip.T)


def solution(mesh):
    placed = (P("ch", "lat", None), P(), P(), P("lat", None, None, None), P(), P("ch", "lat", None))
    return jax.shard_map(
        on_device,
        mesh=mesh,
        in_specs=placed,
        out_specs=(
            P("ch", "lat", None),
            P("ch", "lat", None),
            P("lat", None, None, "ch"),
            P(None, "ch"),
        ),
        check_vma=False,
    )
```
